32 devices in a mesh: groups: 2 (over y), views: 4 (over z), heads: 2 (over x), sub: 2 (over core).
Axes of the slice: x: 2, y: 2, z: 4, core: 2. Of those that a mesh axis runs over, the one named last changes fastest.
Arguments:
- tokens: bfloat16 [4096, 2048], P(('groups', 'views', 'sub'), 'heads'), parts along dimension 0, may hold values from -40 to 40
- w_query: bfloat16 [2048, 2048], P(None, 'heads'), may hold values from -0.125 to 0.125
- w_key: bfloat16 [2048, 2048], P(None, 'heads'), may hold values from -0.125 to 0.125
- w_value: bfloat16 [2048, 2048], P(None, 'heads'), may hold values from -0.125 to 0.125
- w_out: bfloat16 [2048, 2048], P('heads'), may hold values from -0.125 to 0.125
- partners: int32 [64, 20], P(('groups', 'views', 'sub')), parts along dimension 0, may hold values from 0 to 31, as said below
- counts: int32 [64], P(('groups', 'views', 'sub')), parts along dimension 0, may hold values from 6 to 20, as said below
Outputs:
- attended: bfloat16 [4096, 2048], P(('groups', 'views', 'sub'), 'heads'), parts along dimension 0
The draws below stay inside these ranges and needn't reach their ends.
There are 2 independent parts, one for each index of `groups`. The reference program is written for one: setup_inputs(seed, part) draws one part's arguments, and reference() takes and returns one part's arrays. A program takes and returns all parts, laid end to end along the dimension named above; an argument that names none is the same for every part. Nothing has to cross between parts.
Inputs may be any that keep to these rules, and one draw needn't show every extreme that they name: Views lie on a closed orbit of 32 cameras. For t < counts[i], partners[i, t] are distinct views other than i that lie at most 10 views away from i around the orbit (cyclically), in rising order of signed offset; the graph is symmetric; slots t >= counts[i] hold i. `counts`: every view is partnered with the 6 views nearest to it on the orbit; some view has all 20 slots filled in every draw.
All inputs are finite; a program needn't handle non-finite values.
Results may differ from the reference program's by a relative error of at most 0.012.
The reference program's roundings to bfloat16 on the way count: a program that leaves them out, or rounds other values in their place, can miss the bound.
Values may be sent and summed in bfloat16 or wider, within the bound.
No kernel may reach another device: no remote copies, remote signals or barrier semaphores. Data moves between devices by JAX's collectives and lax.ppermute only.
A program may use at most 128 MiB of HBM per device.

```python
import jax
import jax.numpy as jnp
from jax import lax

HEADS = 16
HD = 128
D = 2048
L = 64
R = 10
PMAX = 20
VIEWS = 32


def camera_graph(key):
    key_dense, key_pair, key_center = jax.random.split(jax.random.fold_in(key, 11), 3)
    density = jax.random.randint(key_dense, (VIEWS,), 5, 96)
    rolled = jax.random.randint(key_pair, (VIEWS, R), 0, 100)
    steps = jnp.arange(1, R + 1, dtype=jnp.int32)
    ahead = (jnp.arange(VIEWS, dtype=jnp.int32)[:, None] + steps[None, :]) % VIEWS
    limit = (density[:, None] + density[ahead]) // 2
    present = (rolled < limit) | (steps[None, :] <= 3)
    center = jax.random.randint(key_center, (), 0, VIEWS)
    present = present | (jnp.arange(VIEWS)[:, None] == center) | (ahead == center)
    behind = (jnp.arange(VIEWS, dtype=jnp.int32)[:, None] - steps[None, :]) % VIEWS
    back_present = present[behind, jnp.arange(R)[None, :]]
    full = jnp.concatenate([back_present[:, ::-1], present], axis=1)
    offsets = jnp.concatenate([-steps[::-1], steps])
    others = (jnp.arange(VIEWS, dtype=jnp.int32)[:, None] + offsets[None, :]) % VIEWS
    ranking = jnp.where(full, 0, 1) * (4 * R) + jnp.arange(2 * R, dtype=jnp.int32)[None, :]
    order = jnp.argsort(ranking, axis=1, stable=True)
    sorted_views = jnp.take_along_axis(others, order, axis=1)
    sorted_full = jnp.take_along_axis(full, order, axis=1)
    listed = jnp.where(sorted_full, sorted_views, jnp.arange(VIEWS, dtype=jnp.int32)[:, None])
    return (listed.astype(jnp.int32), jnp.sum(full.astype(jnp.int32), axis=1).astype(jnp.int32))


def draw_partners(key, part):
    listed, number = camera_graph(key)
    return listed


def draw_counts(key, part):
    listed, number = camera_graph(key)
    return number


def draw_tokens(key, part):
    key = jax.random.fold_in(key, 3)
    key_base = jax.random.fold_in(key, 0)
    base = jnp.clip(jax.random.normal(key_base, (VIEWS * L, D), jnp.float32), -4.4, 4.4)
    return base.astype(jnp.bfloat16)


def block_scale(stream_key, shape, cuts, smallest, largest):
    def one(dim, parts):
        heights = jax.random.uniform(jax.random.fold_in(jax.random.fold_in(stream_key, 6), dim), (parts,), jnp.float32, smallest / len(cuts), largest / len(cuts))
        return jnp.repeat(jnp.exp(heights), shape[dim] // parts).reshape((-1,) + (1,) * (len(shape) - dim - 1))

    factor_of = one(*cuts[0])
    for cut in cuts[1:]:
        factor_of = factor_of * one(*cut)
    return factor_of


def noise(rng, extent, scale, most, cuts=(), kind=jnp.bfloat16):
    drawn = jax.random.normal(rng, extent, jnp.float32) * scale
    if len(cuts) > 0:
        drawn = block_scale(rng, extent, cuts, -0.22, 0.18) * drawn
    return jnp.clip(drawn, min=-most, max=most).astype(kind)


def setup_inputs(seed: int = 0, part: int = 0) -> dict:
    key_of = jax.random.split(jax.random.key(seed), 8)
    own_keys = jax.random.split(jax.random.fold_in(key_of[7], part), 8)
    return {
        "tokens": draw_tokens(jax.random.fold_in(jax.random.fold_in(key_of[7], part), 71), part),
        "w_query": noise(key_of[1], (D, D), D ** -0.5, 0.125, ((1, 2),)),
        "w_key": noise(key_of[2], (D, D), D ** -0.5, 0.125, ((1, 2),)),
        "w_value": noise(key_of[3], (D, D), D ** -0.5, 0.125, ((1, 2),)),
        "w_out": noise(key_of[4], (D, D), D ** -0.5, 0.125, ((0, 2),)),
        "partners": draw_partners(jax.random.fold_in(jax.random.fold_in(key_of[7], part), 71), part),
        "counts": draw_counts(jax.random.fold_in(jax.random.fold_in(key_of[7], part), 71), part),
    }


def reference(tokens, w_query, w_key, w_value, w_out, partners, counts):
    scaling = HD ** -0.5
    query = jnp.dot(tokens, w_query, preferred_element_type=jnp.float32).astype(jnp.bfloat16).reshape(VIEWS, L, HEADS, HD)
    keys = jnp.dot(tokens, w_key, preferred_element_type=jnp.float32).astype(jnp.bfloat16).reshape(VIEWS, L, HEADS, HD)
    values = jnp.dot(tokens, w_value, preferred_element_type=jnp.float32).astype(jnp.bfloat16).reshape(VIEWS, L, HEADS, HD)
    slots = jnp.arange(PMAX, dtype=jnp.int32)

    def one_view(view):
        chosen = jnp.concatenate([view[None].astype(jnp.int32), partners[view].astype(jnp.int32)])
        usable = jnp.concatenate([jnp.ones((1,), bool), slots < counts[view]])
        near_keys = keys[chosen].reshape((PMAX + 1) * L, HEADS, HD).astype(jnp.float32)
        near_values = values[chosen].reshape((PMAX + 1) * L, HEADS, HD).astype(jnp.float32)
        scores = jnp.einsum("qhd,khd->hqk", query[view].astype(jnp.float32), near_keys) * scaling
        keep = jnp.repeat(usable, L)
        scores = jnp.where(keep[None, None, :], scores, -jnp.inf)
        top = jnp.max(scores, axis=-1, keepdims=True)
        weights = jnp.where(keep[None, None, :], jnp.exp(scores - top), 0.0)
        weight_sum = jnp.sum(weights, axis=-1)
        rounded = weights.astype(jnp.bfloat16).astype(jnp.float32)
        mixed = jnp.einsum("hqk,khd->hqd", rounded, near_values) / weight_sum[:, :, None]
        return jnp.transpose(mixed, (1, 0, 2)).reshape(L, D).astype(jnp.bfloat16)

    mixed = lax.map(one_view, jnp.arange(VIEWS, dtype=jnp.int32))
    return jnp.dot(mixed.reshape(VIEWS * L, D), w_out, preferred_element_type=jnp.float32).astype(jnp.bfloat16)
```

```python
import functools

import jax
import jax.numpy as jnp
from jax import lax
from jax.experimental import pallas as pl
from jax.experimental.pallas import tpu as pltpu
from jax.sharding import PartitionSpec as P

HD = 128
L = 64
EDGE = 2
MB = 1 << 20


def project_kernel(pieces, side_ref, *refs):
    token_refs, refs = refs[:pieces], refs[pieces:]
    count = len(refs) // 2
    depth = token_refs[0].shape[1]
    for weight_ref, out_ref in zip(refs[:count], refs[count:]):
        total = None
        for step, token_ref in enumerate(token_refs):
            place = lax.rem(side_ref[0] + pieces - step, pieces)
            rows = pl.ds(pl.multiple_of(place * depth, depth), depth)
            term = jnp.dot(token_ref[...], weight_ref[rows, :], preferred_element_type=jnp.float32)
            total = term if total is None else total + term
        out_ref[...] = total.astype(out_ref.dtype)


def project(side, tokens, weights):
    rows, part = tokens[0].shape
    depth, width = weights[0].shape
    tile = min(256, width)
    count = len(weights)
    pieces = len(tokens)
    whole = pl.BlockSpec((rows, part), lambda j, s: (0, 0))
    return pl.pallas_call(
        functools.partial(project_kernel, pieces),
        out_shape=[jax.ShapeDtypeStruct((rows, width), jnp.bfloat16)] * count,
        grid_spec=pltpu.PrefetchScalarGridSpec(
            num_scalar_prefetch=1,
            grid=(width // tile,),
            in_specs=[whole] * pieces
            + [pl.BlockSpec((depth, tile), lambda j, s: (0, j))] * count,
            out_specs=[pl.BlockSpec((rows, tile), lambda j, s: (0, j))] * count,
        ),
        compiler_params=pltpu.CompilerParams(vmem_limit_bytes=24 * MB),
        cost_estimate=pl.CostEstimate(
            flops=2 * rows * depth * width * count,
            bytes_accessed=2 * depth * width * count + 4 * rows * depth,
            transcendentals=0,
        ),
        name="project",
    )(side, *tokens, *weights)


def attend_kernel(sizes, bias_ref, query_ref, *refs):
    count = len(sizes)
    key_refs, value_refs = refs[:count], refs[count : 2 * count]
    out_ref, scores_ref = refs[2 * count :]
    rows = query_ref.shape[0]
    views = rows // L
    query = query_ref[...]
    factor = HD ** (-0.5) * 1.4426950408889634
    top = None
    start = 0
    for key_ref, size in zip(key_refs, sizes):
        scores = lax.dot_general(
            query, key_ref[...], (((1,), (1,)), ((), ())), preferred_element_type=jnp.float32
        )
        scores = scores.reshape(views, L, size) + bias_ref[:, start : start + size][:, None, :]
        scores = scores.reshape(rows, size)
        scores_ref[:, start : start + size] = scores
        for part in range(0, size, 128):
            piece = scores[:, part : part + 128]
            top = piece if top is None else jnp.maximum(top, piece)
        start += size
    top = jnp.max(top, axis=1, keepdims=True)
    total = jnp.zeros((rows, 128), jnp.float32)
    mixed = jnp.zeros((rows, HD), jnp.float32)
    start = 0
    for value_ref, size in zip(value_refs, sizes):
        weights = jnp.exp2((scores_ref[:, start : start + size] - top) * factor)
        for part in range(0, size, 128):
            total += weights[:, part : part + 128]
        mixed += jnp.dot(
            weights.astype(jnp.bfloat16), value_ref[...], preferred_element_type=jnp.float32
        )
        start += size
    out_ref[...] = (mixed / jnp.sum(total, axis=1, keepdims=True)).astype(out_ref.dtype)


def attend(bias, query, pairs):
    rows, width = query.shape
    sizes = tuple(keys.shape[0] for keys, _ in pairs)
    span = sum(sizes)
    heads = width // HD
    column = lambda size: pl.BlockSpec((size, HD), lambda h: (0, h))
    return pl.pallas_call(
        functools.partial(attend_kernel, sizes),
        out_shape=jax.ShapeDtypeStruct((rows, width), jnp.bfloat16),
        grid=(heads,),
        in_specs=[pl.BlockSpec(bias.shape, lambda h: (0, 0)), column(rows)]
        + [column(size) for size in sizes] * 2,
        out_specs=column(rows),
        scratch_shapes=[pltpu.VMEM((rows, span), jnp.float32)],
        compiler_params=pltpu.CompilerParams(vmem_limit_bytes=24 * MB),
        cost_estimate=pl.CostEstimate(
            flops=4 * rows * span * width,
            bytes_accessed=4 * span * width,
            transcendentals=rows * span * heads,
        ),
        name="attend",
    )(bias, query, *[keys for keys, _ in pairs], *[values for _, values in pairs])


def output_kernel(side_ref, mixed_ref, weight_ref, out_ref):
    out_ref[...] = jnp.dot(
        mixed_ref[...], weight_ref[...], preferred_element_type=jnp.float32
    ).astype(out_ref.dtype)


def output_part(place, sides, mixed, weight, dtype):
    rows, depth = mixed.shape
    part = weight.shape[1] // sides
    tile = min(256, part)
    steps = part // tile
    return pl.pallas_call(
        output_kernel,
        out_shape=jax.ShapeDtypeStruct((rows, part), dtype),
        grid_spec=pltpu.PrefetchScalarGridSpec(
            num_scalar_prefetch=1,
            grid=(steps,),
            in_specs=[
                pl.BlockSpec((rows, depth), lambda j, s: (0, 0)),
                pl.BlockSpec((depth, tile), lambda j, s: (0, s[0] * steps + j)),
            ],
            out_specs=pl.BlockSpec((rows, tile), lambda j, s: (0, j)),
        ),
        compiler_params=pltpu.CompilerParams(vmem_limit_bytes=24 * MB),
        cost_estimate=pl.CostEstimate(
            flops=2 * rows * depth * part, bytes_accessed=2 * depth * part, transcendentals=0
        ),
        name="output_part",
    )(place, mixed, weight)


def shards(tokens, w_query, w_key, w_value, w_out, partners, counts):
    rows = tokens.shape[0]
    views_here = rows // L
    chips = lax.axis_size("views")
    cores = lax.axis_size("sub")
    total_views = views_here * chips * cores
    place = lax.axis_index("views")
    core = lax.axis_index("sub")
    sides = lax.axis_size("heads")
    side = lax.axis_index("heads").astype(jnp.int32).reshape(1)

    def shift(a, step):
        return lax.ppermute(a, "heads", [(h, (h + step) % sides) for h in range(sides)])

    def gather(a):
        return [a] + [shift(a, step) for step in range(1, sides)]

    share = lambda a: lax.ppermute(a, "sub", [(0, 1), (1, 0)])
    pair = [(z, z ^ 1) for z in range(chips)]
    side_step = [(z, ((z - 1) if z % 2 == 0 else (z + 1)) % chips) for z in range(chips)]
    edge = [(2 * z + 1, 2 * ((z + 2) % chips)) for z in range(chips)]
    edge += [(2 * z, 2 * ((z - 2) % chips) + 1) for z in range(chips)]

    edge_rows = EDGE * L
    first = lax.slice_in_dim(tokens, 0, edge_rows, axis=0)
    last = lax.slice_in_dim(tokens, rows - edge_rows, rows, axis=0)
    own_pieces = gather(tokens)
    near = lax.ppermute(tokens, "views", pair)
    next_near = lax.ppermute(tokens, "views", side_step)
    rim = lax.ppermute(jnp.where(core == 0, first, last), ("views", "sub"), edge)

    query, own_keys, own_values = project(side, own_pieces, (w_query, w_key, w_value))
    own = (own_keys, own_values)
    near_kv = project(side, gather(near), (w_key, w_value))
    next_kv = project(side, gather(next_near), (w_key, w_value))
    rim_kv = project(side, gather(rim), (w_key, w_value))

    pairs = []
    bases = []
    even = place % 2 == 0
    near_place = place ^ 1
    next_place = jnp.where(even, place - 1, place + 1) % chips
    for kv, at in ((own, place), (near_kv, near_place), (next_kv, next_place)):
        pairs.append(tuple(kv))
        bases.append((at * cores + core) * views_here + jnp.arange(views_here, dtype=jnp.int32))
        pairs.append(tuple(share(a) for a in kv))
        bases.append((at * cores + 1 - core) * views_here + jnp.arange(views_here, dtype=jnp.int32))
    pairs.append(tuple(rim_kv))
    far_first = jnp.where(
        core == 0,
        ((place - 2) * cores + 1) * views_here + views_here - EDGE,
        (place + 2) * cores * views_here,
    )
    bases.append((far_first + jnp.arange(EDGE, dtype=jnp.int32)) % total_views)
    listed = jnp.concatenate(bases)

    mine = (place * cores + core) * views_here + jnp.arange(views_here, dtype=jnp.int32)
    slots = jnp.arange(partners.shape[1], dtype=jnp.int32)
    valid = slots[None, :] < counts[:, None]
    allowed = jnp.any(
        valid[:, :, None] & (partners[:, :, None] == listed[None, None, :]), axis=1
    ) | (mine[:, None] == listed[None, :])
    bias = jnp.repeat(jnp.where(allowed, 0.0, -1e30).astype(jnp.float32), L, axis=1)

    mixed = attend(bias, query, pairs)
    total = None
    for step in range(1, sides):
        sent = output_part((side + step) % sides, sides, mixed, w_out, jnp.bfloat16)
        term = shift(sent, step).astype(jnp.float32)
        total = term if total is None else total + term
    kept = output_part(side, sides, mixed, w_out, jnp.float32)
    return (kept + total).astype(jnp.bfloat16)


def solution(mesh):
    in_specs = (
        P(("groups", "views", "sub"), "heads"),
        P(None, "heads"),
        P(None, "heads"),
        P(None, "heads"),
        P("heads", None),
        P(("groups", "views", "sub"), None),
        P(("groups", "views", "sub")),
    )
    out_specs = P(("groups", "views", "sub"), "heads")
    return jax.shard_map(shards, mesh=mesh, in_specs=in_specs, out_specs=out_specs, check_vma=False)
```

```python
import functools

import jax
import jax.numpy as jnp
from jax import lax
from jax.experimental import pallas as pl
from jax.experimental.pallas import tpu as pltpu
from jax.sharding import PartitionSpec as P

HD = 128
L = 64
EDGE = 2
MB = 1 << 20
FACTOR = HD ** (-0.5) * 1.4426950408889634
ROWS_BY_ROWS = (((1,), (1,)), ((), ()))

VMEM = pl.BlockSpec(memory_space=pltpu.VMEM)
SMEM = pl.BlockSpec(memory_space=pltpu.SMEM)
HBM = pl.BlockSpec(memory_space=pl.ANY)
PLACE, CORE, SIDE = range(3)


def call(kernel, outs, ins, scratch=(), name=None, out_specs=None, aliases=None, whole=()):
    return pl.pallas_call(
        kernel,
        out_shape=outs,
        in_specs=[
            HBM if k in whole else SMEM if a.dtype == jnp.int32 and a.ndim == 1 else VMEM
            for k, a in enumerate(ins)
        ],
        out_specs=jax.tree.map(lambda _: VMEM, outs) if out_specs is None else out_specs,
        scratch_shapes=list(scratch),
        input_output_aliases=aliases or {},
        compiler_params=pltpu.CompilerParams(vmem_limit_bytes=16 * MB),
        cost_estimate=pl.CostEstimate(flops=0, bytes_accessed=0, transcendentals=0),
        name=name,
    )(*ins)


def after(a, *others):
    return lax.optimization_barrier((a, *others))[0]


def prepare_kernel(chips, cores, here_ref, counts_ref, partners_ref, *refs):
    w_query_ref, w_value_ref, w_key_ref, w_out_ref, turned_query_ref, turned_value_ref, bias_ref = refs
    step = 256
    for weight_ref, turned_ref in ((w_query_ref, turned_query_ref), (w_value_ref, turned_value_ref)):
        for start in range(0, weight_ref.shape[0], step):
            turned_ref[:, start : start + step] = weight_ref[start : start + step, :].T

    views, width = partners_ref.shape
    total = views * chips * cores
    place, core = here_ref[PLACE], here_ref[CORE]
    near = place + 1 - 2 * lax.rem(place, 2)
    beyond = lax.rem(place + chips - 1 + 2 * lax.rem(place, 2), chips)
    bases = []
    for at in (place, near, beyond):
        bases.append((at * cores + core) * views)
        bases.append((at * cores + 1 - core) * views)
    behind = (lax.rem(place + chips - 2, chips) * cores + 1) * views + views - EDGE
    ahead = lax.rem(place + 2, chips) * cores * views
    bases.append(jnp.where(core == 0, behind, ahead))
    rows = bias_ref.shape[0]
    row = lax.broadcasted_iota(jnp.int32, (rows, width), 0)
    listed = row + bases[0]
    for block in range(1, len(bases)):
        listed = jnp.where(row >= block * views, row - block * views + bases[block], listed)
    slot = lax.broadcasted_iota(jnp.int32, (rows, width), 1)
    for view in range(views):
        mine = (place * cores + core) * views + view
        hit = (partners_ref[view : view + 1, :] == listed) & (slot < counts_ref[view])
        hit = jnp.where(hit | (listed == mine), 1, 0)
        hit = jnp.max(hit, axis=1, keepdims=True)
        mask = jnp.where(hit > 0, 0.0, -1e30).astype(jnp.float32)
        bias_ref[:, view * L : view * L + L] = jnp.broadcast_to(mask, (rows, L))


def prepare(chips, cores, here, counts, partners, w_query, w_value, w_key, w_out):
    depth, width = w_value.shape
    views = partners.shape[0]
    turned = jax.ShapeDtypeStruct((width, depth), w_value.dtype)
    return call(
        functools.partial(prepare_kernel, chips, cores),
        [turned, turned, jax.ShapeDtypeStruct((6 * views + EDGE, views * L), jnp.float32)],
        [here, counts, partners, w_query, w_value, w_key, w_out],
        name="prepare",
    )


def project_kernel(pieces, parts, with_query, here_ref, *refs):
    token_refs, refs = refs[:pieces], refs[pieces:]
    depth = token_refs[0].shape[1]
    spans = []
    for step in range(pieces):
        place = lax.rem(here_ref[SIDE] + pieces - step, pieces)
        spans.append(pl.ds(pl.multiple_of(place * depth, depth), depth))

    def plain(weight_ref, out_refs):
        width = weight_ref.shape[1]
        tile = min(512, width)
        for start in range(0, width, tile):
            total = None
            for token_ref, span in zip(token_refs, spans):
                term = jnp.dot(
                    token_ref[...],
                    weight_ref[span, start : start + tile],
                    preferred_element_type=jnp.float32,
                )
                total = term if total is None else total + term
            total = total.astype(jnp.bfloat16)
            for index, out_ref in enumerate(out_refs):
                size = out_ref.shape[0]
                out_ref[:, start : start + tile] = total[index * size : index * size + size]

    def turned(weight_ref, out_refs):
        width = weight_ref.shape[0]
        tile = min(512, width)
        for start in range(0, width, tile):
            total = None
            for token_ref, span in zip(token_refs, spans):
                term = lax.dot_general(
                    weight_ref[start : start + tile, span],
                    token_ref[...],
                    ROWS_BY_ROWS,
                    preferred_element_type=jnp.float32,
                )
                total = term if total is None else total + term
            total = total.astype(jnp.bfloat16)
            for index, out_ref in enumerate(out_refs):
                size = out_ref.shape[1]
                out_ref[start : start + tile, :] = total[:, index * size : index * size + size]

    weights, outs = refs[: 2 + with_query], refs[2 + with_query :]
    plain(weights[0], outs[:parts])
    turned(weights[1], outs[parts : 2 * parts])
    if with_query:
        turned(weights[2], outs[2 * parts :])


def project(here, tokens, w_key, w_value, w_query=None, parts=1):
    rows = tokens[0].shape[0]
    width = w_key.shape[1]
    weights = [w_key, w_value] + ([] if w_query is None else [w_query])
    outs = [jax.ShapeDtypeStruct((rows // parts, width), jnp.bfloat16)] * parts
    outs += [jax.ShapeDtypeStruct((width, rows // parts), jnp.bfloat16)] * parts
    if w_query is not None:
        outs += [jax.ShapeDtypeStruct((width, rows), jnp.bfloat16)]
    outs = call(
        functools.partial(project_kernel, len(tokens), parts, w_query is not None),
        outs,
        [here, *tokens, *weights],
        name="project",
    )
    return list(zip(outs[:parts], outs[parts : 2 * parts])), outs[2 * parts :]


def scores_of(key_ref, first, last, query, column, bias_ref, bias_row, lanes, hold_ref, at, top):
    scores = jnp.dot(key_ref[first:last, column], query, preferred_element_type=jnp.float32)
    for view in range((last - first) // L):
        piece = scores[view * L : view * L + L] + bias_ref[bias_row + view : bias_row + view + 1, lanes]
        hold_ref[at + view * L : at + view * L + L, :] = piece
        best = jnp.max(piece.reshape(L // 8, 8, piece.shape[1]), axis=0)
        top = best if top is None else jnp.maximum(top, best)
    return top


def weigh(hold_ref, at, size, shift, value, total, mixed):
    weights = jnp.exp2(hold_ref[at : at + size, :] * FACTOR - shift)
    term = jnp.sum(weights.reshape(size // 8, 8, weights.shape[1]), axis=0)
    total = term if total is None else total + term
    update = jnp.dot(value, weights.astype(jnp.bfloat16), preferred_element_type=jnp.float32)
    mixed = update if mixed is None else mixed + update
    return total, mixed


def attend_kernel(blocks, bias_start, has_state, bias_ref, query_ref, *refs):
    key_refs, value_refs = refs[:blocks], refs[blocks : 2 * blocks]
    refs = refs[2 * blocks :]
    if has_state:
        top_in, total_in, mixed_in, top_out, total_out, mixed_out, hold = refs
    else:
        top_out, total_out, mixed_out, hold = refs
    heads = query_ref.shape[0] // HD
    everything = slice(None)
    for head in range(heads):
        column = slice(head * HD, head * HD + HD)
        row = slice(head, head + 1)
        query = query_ref[column, :]
        slot = hold.at[head % 2]
        top, at, groups = None, 0, []
        for index, key_ref in enumerate(key_refs):
            size = key_ref.shape[0]
            step = min(128, size)
            for first in range(0, size, step):
                top = scores_of(
                    key_ref, first, first + step, query, column,
                    bias_ref, bias_start + at // L, everything, slot, at, top,
                )
                if at % 256 == 0:
                    groups.append((at, []))
                groups[-1][1].append((index, first, step))
                at += step
        top = jnp.max(top, axis=0, keepdims=True)
        total = mixed = None
        if has_state:
            before = top_in[row, :]
            top = jnp.maximum(top, before)
        shift = top * FACTOR
        for at, group in groups:
            value = jnp.concatenate(
                [value_refs[i][column, first : first + step] for i, first, step in group], axis=1
            )
            total, mixed = weigh(slot, at, value.shape[1], shift, value, total, mixed)
        total = jnp.sum(total, axis=0, keepdims=True)
        if has_state:
            keep = jnp.exp2(before * FACTOR - shift)
            total = total + total_in[row, :] * keep
            mixed = mixed + mixed_in[column, :] * keep
        top_out[row, :] = top
        total_out[row, :] = total
        mixed_out[column, :] = mixed


def attend(bias, bias_start, query, blocks, state):
    width, rows = query.shape
    heads = width // HD
    span = sum(keys.shape[0] for keys, _ in blocks)
    outs = [
        jax.ShapeDtypeStruct((heads, rows), jnp.float32),
        jax.ShapeDtypeStruct((heads, rows), jnp.float32),
        jax.ShapeDtypeStruct((width, rows), jnp.float32),
    ]
    keys, values = [k for k, _ in blocks], [v for _, v in blocks]
    return call(
        functools.partial(attend_kernel, len(blocks), bias_start, state is not None),
        outs,
        [bias, query, *keys, *values, *(state or [])],
        scratch=[pltpu.VMEM((2, span, rows), jnp.float32)],
        name="attend",
    )


def finish_kernel(sides, bias_start, inner, has_rim, here_ref, top_ref, total_ref, mixed_ref, *refs):
    if has_rim:
        bias_ref, query_ref, key_ref, value_ref, weight_ref = refs[:5]
        refs = refs[5:]
        hold = refs[-1]
    else:
        weight_ref = refs[0]
        refs = refs[1:]
    sent_refs, kept_ref, done = refs[: sides - 1], refs[sides - 1], refs[sides]
    rows = kept_ref.shape[0]
    part = kept_ref.shape[1]
    spot = spot_of(here_ref, inner, rows, mixed_ref.shape[1])
    heads = mixed_ref.shape[0] // HD
    for head in range(heads):
        column = slice(head * HD, head * HD + HD)
        row = slice(head, head + 1)
        total = total_ref[row, spot]
        mixed = mixed_ref[column, spot]
        if has_rim:
            slot = hold.at[head % 2]
            size = key_ref.shape[0]
            before = top_ref[row, spot]
            top = scores_of(
                key_ref, 0, size, query_ref[column, spot], column,
                bias_ref, bias_start, spot, slot, 0, None,
            )
            top = jnp.maximum(jnp.max(top, axis=0, keepdims=True), before)
            shift = top * FACTOR
            more, update = weigh(slot, 0, size, shift, value_ref[column, :], None, None)
            keep = jnp.exp2(before * FACTOR - shift)
            total = total * keep + jnp.sum(more, axis=0, keepdims=True)
            mixed = mixed * keep + update
        done[:, column] = (mixed / total).T.astype(done.dtype)
    for step in range(sides):
        step = (step + 1) % sides
        place = lax.rem(here_ref[SIDE] + step, sides)
        columns = pl.ds(pl.multiple_of(place * part, part), part)
        result = jnp.dot(done[...], weight_ref[:, columns], preferred_element_type=jnp.float32)
        if step == 0:
            kept_ref[...] = result
        else:
            sent_refs[step - 1][...] = result.astype(jnp.bfloat16)


def spot_of(here_ref, inner, size, rows):
    late = 1 - here_ref[CORE] if inner else here_ref[CORE]
    return pl.ds(pl.multiple_of(late * (rows - size), L), size)


def finish(sides, here, inner, rows, state, weight, rim=None):
    top, total, mixed = state
    width = mixed.shape[0]
    part = weight.shape[1] // sides
    outs = [jax.ShapeDtypeStruct((rows, part), jnp.bfloat16)] * (sides - 1)
    outs += [jax.ShapeDtypeStruct((rows, part), jnp.float32)]
    scratch = [pltpu.VMEM((rows, width), jnp.bfloat16)]
    ins = [here, top, total, mixed]
    bias_start = 0
    if rim is not None:
        bias, bias_start, query, keys, values = rim
        ins += [bias, query, keys, values]
        scratch += [pltpu.VMEM((2, keys.shape[0], rows), jnp.float32)]
    return call(
        functools.partial(finish_kernel, sides, bias_start, inner, rim is not None),
        outs,
        ins + [weight],
        scratch=scratch,
        name="finish",
    )


def settle_kernel(inner, count, here_ref, *refs):
    kept_ref, term_refs = refs[0], refs[1:count]
    out_ref, hold, sem = refs[-3:]
    total = kept_ref[...]
    for term_ref in term_refs:
        total += term_ref[...].astype(jnp.float32)
    hold[...] = total.astype(hold.dtype)
    rows = hold.shape[0]
    spot = spot_of(here_ref, inner, rows, out_ref.shape[0])
    copy = pltpu.make_async_copy(hold, out_ref.at[spot, :], sem)
    copy.start()
    copy.wait()


def settle(here, inner, parts, rows, before=None):
    size, width = parts[0].shape
    ins = [here, *parts] + ([] if before is None else [before])
    return call(
        functools.partial(settle_kernel, inner, len(parts)),
        jax.ShapeDtypeStruct((rows, width), jnp.bfloat16),
        ins,
        scratch=[pltpu.VMEM((size, width), jnp.bfloat16), pltpu.SemaphoreType.DMA],
        out_specs=HBM,
        whole=() if before is None else (len(ins) - 1,),
        aliases=None if before is None else {len(ins) - 1: 0},
        name="settle",
    )


def shards(tokens, w_query, w_key, w_value, w_out, partners, counts):
    rows = tokens.shape[0]
    views_here = rows // L
    chips = lax.axis_size("views")
    cores = lax.axis_size("sub")
    sides = lax.axis_size("heads")
    core = lax.axis_index("sub")
    here = jnp.stack([lax.axis_index(name) for name in ("views", "sub", "heads")]).astype(jnp.int32)

    def shift(a, step):
        return lax.ppermute(a, "heads", [(h, (h + step) % sides) for h in range(sides)])

    def gather(a):
        return [a] + [shift(a, step) for step in range(1, sides)]

    def share(blocks):
        return [tuple(lax.ppermute(a, "sub", [(0, 1), (1, 0)]) for a in block) for block in blocks]

    pair = [(z, z ^ 1) for z in range(chips)]
    side_step = [(z, ((z - 1) if z % 2 == 0 else (z + 1)) % chips) for z in range(chips)]
    edge = [(2 * z + 1, 2 * ((z + 2) % chips)) for z in range(chips)]
    edge += [(2 * z, 2 * ((z - 2) % chips) + 1) for z in range(chips)]

    edge_rows = EDGE * L
    rim = lax.dynamic_slice_in_dim(tokens, core * (rows - edge_rows), edge_rows, axis=0)
    here = after(here, rim)
    own = gather(tokens)
    near = lax.ppermute(tokens, "views", pair)
    beyond = lax.ppermute(tokens, "views", side_step)
    w_query, w_value, bias = prepare(
        chips, cores, here, counts, partners, w_query, w_value, w_key, w_out
    )
    rim = lax.ppermute(after(rim, own[1]), ("views", "sub"), edge)

    own_blocks, (query,) = project(here, own, w_key, w_value, w_query, 2)
    own_shared = share(own_blocks)
    state = attend(bias, 0, query, own_blocks + own_shared[:1], None)
    near = gather(near)
    beyond = gather(after(beyond, state[0]))
    near_blocks, _ = project(here, near, w_key, w_value)
    near_shared = share(near_blocks)
    state = attend(bias, views_here + 2, query, own_shared[1:] + near_blocks, state)
    rim = gather(rim)
    beyond[1] = after(beyond[1], state[0], rim[0])
    beyond_blocks, _ = project(here, beyond, w_key, w_value)
    beyond_shared = share([(after(beyond_blocks[0][0], rim[1]), beyond_blocks[0][1])])
    state = attend(bias, 3 * views_here, query, near_shared + beyond_blocks, state)
    ((rim_keys, rim_values),), _ = project(here, rim, w_key, w_value)
    state = attend(bias, 5 * views_here, query, beyond_shared, state)

    inner = finish(sides, here, True, rows - edge_rows, state, w_out)
    outer = finish(
        sides, here, False, edge_rows, [after(state[0], inner[0]), *state[1:]], w_out,
        (bias, 6 * views_here, query, rim_keys, rim_values),
    )

    def exchange(parts):
        return [parts[-1]] + [shift(part, step + 1) for step, part in enumerate(parts[:-1])]

    inner, outer = exchange(inner), exchange(outer)
    attended = settle(here, True, inner, rows)
    return settle(here, False, outer, rows, attended)


def solution(mesh):
    in_specs = (
        P(("groups", "views", "sub"), "heads"),
        P(None, "heads"),
        P(None, "heads"),
        P(None, "heads"),
        P("heads", None),
        P(("groups", "views", "sub"), None),
        P(("groups", "views", "sub")),
    )
    out_specs = P(("groups", "views", "sub"), "heads")
    return jax.shard_map(shards, mesh=mesh, in_specs=in_specs, out_specs=out_specs, check_vma=False)
```

```python
import functools

import jax
import jax.numpy as jnp
from jax import lax
from jax.experimental import pallas as pl
from jax.experimental.pallas import tpu as pltpu
from jax.sharding import PartitionSpec as P

HD = 128
L = 64
EDGE = 2
MB = 1 << 20
FAKE = 300_000_000
FACTOR = HD ** (-0.5) * 1.4426950408889634
ROWS_BY_ROWS = (((1,), (1,)), ((), ()))

VMEM = pl.BlockSpec(memory_space=pltpu.VMEM)
SMEM = pl.BlockSpec(memory_space=pltpu.SMEM)
HBM = pl.BlockSpec(memory_space=pl.ANY)
PLACE, CORE, SIDE = range(3)


def call(kernel, outs, ins, scratch=(), name=None, out_specs=None, aliases=None, whole=(), flops=0):
    return pl.pallas_call(
        kernel,
        out_shape=outs,
        in_specs=[
            HBM if k in whole else SMEM if a.dtype == jnp.int32 and a.ndim == 1 else VMEM
            for k, a in enumerate(ins)
        ],
        out_specs=jax.tree.map(lambda _: VMEM, outs) if out_specs is None else out_specs,
        scratch_shapes=list(scratch),
        input_output_aliases=aliases or {},
        compiler_params=pltpu.CompilerParams(vmem_limit_bytes=16 * MB),
        cost_estimate=pl.CostEstimate(flops=flops, bytes_accessed=0, transcendentals=0),
        name=name,
    )(*ins)


def after(a, *others):
    return lax.optimization_barrier((a, *others))[0]


def mask_kernel(chips, cores, here_ref, counts_ref, partners_ref, *refs):
    bias_ref = refs[-1]
    views, width = partners_ref.shape
    total = views * chips * cores
    place, core = here_ref[PLACE], here_ref[CORE]
    near = place + 1 - 2 * lax.rem(place, 2)
    beyond = lax.rem(place + chips - 1 + 2 * lax.rem(place, 2), chips)
    bases = []
    for at, other in ((place, 0), (near, 0), (near, 1), (place, 1), (beyond, 0), (beyond, 1)):
        bases.append((at * cores + core * (1 - 2 * other) + other) * views)
    behind = (lax.rem(place + chips - 2, chips) * cores + 1) * views + views - EDGE
    ahead = lax.rem(place + 2, chips) * cores * views
    bases.append(jnp.where(core == 0, behind, ahead))
    rows = bias_ref.shape[0]
    row = lax.broadcasted_iota(jnp.int32, (rows, width), 0)
    listed = row + bases[0]
    for block in range(1, len(bases)):
        listed = jnp.where(row >= block * views, row - block * views + bases[block], listed)
    slot = lax.broadcasted_iota(jnp.int32, (rows, width), 1)
    for view in range(views):
        mine = (place * cores + core) * views + view
        hit = (partners_ref[view : view + 1, :] == listed) & (slot < counts_ref[view])
        hit = jnp.where(hit | (listed == mine), 1, 0)
        hit = jnp.max(hit, axis=1, keepdims=True)
        mask = jnp.where(hit > 0, 0.0, -1e30).astype(jnp.float32)
        bias_ref[:, view * L : view * L + L] = jnp.broadcast_to(mask, (rows, L))


def fetch_kernel(*refs):
    refs[-1][...] = jnp.zeros_like(refs[-1])


def fetch(*arrays, flops=0):
    return call(
        fetch_kernel, jax.ShapeDtypeStruct((8, 128), jnp.float32), arrays, name="fetch", flops=flops
    )


def make_mask(chips, cores, here, counts, partners, fetched):
    views = partners.shape[0]
    return call(
        functools.partial(mask_kernel, chips, cores),
        jax.ShapeDtypeStruct((6 * views + EDGE, views * L), jnp.float32),
        [here, counts, partners, fetched],
        name="mask",
    )


def project_kernel(pieces, groups, parts, with_query, here_ref, *refs):
    token_refs, refs = refs[: pieces * groups], refs[pieces * groups :]
    token_refs = [token_refs[k * groups : k * groups + groups] for k in range(pieces)]
    depth = token_refs[0][0].shape[1]
    spans = []
    for step in range(pieces):
        place = lax.rem(here_ref[SIDE] + pieces - step, pieces)
        spans.append(pl.ds(pl.multiple_of(place * depth, depth), depth))

    def products(weight_ref):
        width = weight_ref.shape[1]
        tile = min(512, width)
        for start in range(0, width, tile):
            total = None
            for group_refs, span in zip(token_refs, spans):
                term = jnp.dot(
                    jnp.concatenate([ref[...] for ref in group_refs]),
                    weight_ref[span, start : start + tile],
                    preferred_element_type=jnp.float32,
                )
                total = term if total is None else total + term
            yield start, total.astype(jnp.bfloat16)

    rows = sum(ref.shape[0] for ref in token_refs[0])
    block_refs, refs = refs[2 + with_query : 2 + with_query + parts], refs[:2 + with_query] + refs[2 + with_query + parts :]
    key_ref, value_ref = halves_of(block_refs)
    for start, result in products(refs[0]):
        key_ref[:, start : start + result.shape[1]] = result
    for start, result in products(refs[1]):
        for column in range(0, result.shape[1], HD):
            at, keys = value_place((start + column) // HD, rows)
            value_ref[at, keys] = result[:, column : column + HD].T
    if with_query:
        for start, result in products(refs[2]):
            refs[3][start : start + result.shape[1], :] = result.T


def value_place(head, keys):
    deep = keys // HD
    first = head % deep * HD
    return slice(first, first + HD), slice(head // deep * keys, head // deep * keys + keys)


def halves_of(block_refs):
    if len(block_refs) == 2:
        return block_refs
    rows = block_refs[0].shape[0] // 2
    return block_refs[0].at[:rows], block_refs[0].at[rows:]


def project(here, tokens, w_key, w_value, w_query=None, parts=2):
    rows = sum(a.shape[0] for a in tokens[0])
    width = w_key.shape[1]
    weights = [w_key, w_value] + ([] if w_query is None else [w_query])
    outs = [jax.ShapeDtypeStruct((2 * rows // parts, width), jnp.bfloat16)] * parts
    if w_query is not None:
        outs += [jax.ShapeDtypeStruct((width, rows), jnp.bfloat16)]
    outs = call(
        functools.partial(project_kernel, len(tokens), len(tokens[0]), parts, w_query is not None),
        outs,
        [here, *[a for piece in tokens for a in piece], *weights],
        name="project",
    )
    return (tuple(outs[:parts]), *outs[parts:])


def scores_of(key_ref, first, last, query, column, bias_ref, bias_row, lanes, hold_ref, at, top):
    scores = jnp.dot(key_ref[first:last, column], query, preferred_element_type=jnp.float32)
    for view in range((last - first) // L):
        piece = scores[view * L : view * L + L] + bias_ref[bias_row + view : bias_row + view + 1, lanes]
        hold_ref[at + view * L : at + view * L + L, :] = piece
        best = jnp.max(piece.reshape(L // 8, 8, piece.shape[1]), axis=0)
        top = best if top is None else jnp.maximum(top, best)
    return top


def weigh(hold_ref, at, size, shift, value, total, mixed):
    weights = jnp.exp2(hold_ref[at : at + size, :] * FACTOR - shift)
    term = jnp.sum(weights.reshape(size // 8, 8, weights.shape[1]), axis=0)
    total = term if total is None else total + term
    update = jnp.dot(value, weights.astype(jnp.bfloat16), preferred_element_type=jnp.float32)
    mixed = update if mixed is None else mixed + update
    return total, mixed


def attend_kernel(blocks, bias_start, has_state, bias_ref, query_ref, *refs):
    pairs = []
    for parts in blocks:
        pairs.append(halves_of(refs[:parts]))
        refs = refs[parts:]
    if has_state:
        top_in, total_in, mixed_in, top_out, total_out, mixed_out, hold = refs
    else:
        top_out, total_out, mixed_out, hold = refs
    heads = query_ref.shape[0] // HD
    everything = slice(None)
    for head in range(heads):
        column = slice(head * HD, head * HD + HD)
        row = slice(head, head + 1)
        query = query_ref[column, :]
        slot = hold.at[head % 2]
        top, at, groups = None, 0, []
        for key_ref, value_ref in pairs:
            size = key_ref.shape[0]
            step = min(128, size)
            groups.append((at, size, value_ref))
            for first in range(0, size, step):
                top = scores_of(
                    key_ref, first, first + step, query, column,
                    bias_ref, bias_start + at // L, everything, slot, at, top,
                )
                at += step
        top = jnp.max(top, axis=0, keepdims=True)
        total = mixed = None
        if has_state:
            before = top_in[row, :]
            top = jnp.maximum(top, before)
        shift = top * FACTOR
        for at, size, value_ref in groups:
            value = value_ref[value_place(head, size)]
            total, mixed = weigh(slot, at, size, shift, value, total, mixed)
        total = jnp.sum(total, axis=0, keepdims=True)
        if has_state:
            keep = jnp.exp2(before * FACTOR - shift)
            total = total + total_in[row, :] * keep
            mixed = mixed + mixed_in[column, :] * keep
        top_out[row, :] = top
        total_out[row, :] = total
        mixed_out[column, :] = mixed


def attend(bias, bias_start, query, blocks, state, flops=0):
    width, rows = query.shape
    heads = width // HD
    span = sum(a.shape[0] for block in blocks for a in block) // 2
    outs = [
        jax.ShapeDtypeStruct((heads, rows), jnp.float32),
        jax.ShapeDtypeStruct((heads, rows), jnp.float32),
        jax.ShapeDtypeStruct((width, rows), jnp.float32),
    ]
    return call(
        functools.partial(attend_kernel, [len(block) for block in blocks], bias_start, state is not None),
        outs,
        [bias, query, *[a for block in blocks for a in block], *(state or [])],
        scratch=[pltpu.VMEM((2, span, rows), jnp.float32)],
        name="attend",
        flops=flops,
    )


def finish_kernel(sides, bias_start, inner, has_rim, here_ref, top_ref, total_ref, mixed_ref, *refs):
    if has_rim:
        bias_ref, query_ref, key_ref, value_ref, weight_ref = refs[:5]
        refs = refs[5:]
        hold = refs[-1]
    else:
        weight_ref = refs[0]
        refs = refs[1:]
    sent_refs, kept_ref, done = refs[: sides - 1], refs[sides - 1], refs[sides]
    rows = kept_ref.shape[0]
    part = kept_ref.shape[1]
    spot = spot_of(here_ref, inner, rows, mixed_ref.shape[1])
    heads = mixed_ref.shape[0] // HD
    for head in range(heads):
        column = slice(head * HD, head * HD + HD)
        row = slice(head, head + 1)
        total = total_ref[row, spot]
        mixed = mixed_ref[column, spot]
        if has_rim:
            slot = hold.at[head % 2]
            size = key_ref.shape[0]
            before = top_ref[row, spot]
            top = scores_of(
                key_ref, 0, size, query_ref[column, spot], column,
                bias_ref, bias_start, spot, slot, 0, None,
            )
            top = jnp.maximum(jnp.max(top, axis=0, keepdims=True), before)
            shift = top * FACTOR
            value = value_ref[value_place(head, size)]
            more, update = weigh(slot, 0, size, shift, value, None, None)
            keep = jnp.exp2(before * FACTOR - shift)
            total = total * keep + jnp.sum(more, axis=0, keepdims=True)
            mixed = mixed * keep + update
        done[:, column] = (mixed / total).T.astype(done.dtype)
    for step in range(sides):
        step = (step + 1) % sides
        place = lax.rem(here_ref[SIDE] + step, sides)
        columns = pl.ds(pl.multiple_of(place * part, part), part)
        result = jnp.dot(done[...], weight_ref[:, columns], preferred_element_type=jnp.float32)
        if step == 0:
            kept_ref[...] = result
        else:
            sent_refs[step - 1][...] = result.astype(jnp.bfloat16)


def pick_kernel(here_ref, inner_ref, outer_ref, fetched_ref, block_ref, edge_ref):
    place = here_ref[PLACE]
    is_inner = (place == 1) | (place == 2)

    def take(chosen_ref):
        block_ref[...] = chosen_ref[...]
        rows = spot_of(here_ref, False, edge_ref.shape[0], chosen_ref.shape[0])
        edge_ref[...] = chosen_ref[rows, :]

    @pl.when(is_inner)
    def _():
        take(inner_ref)

    @pl.when(jnp.logical_not(is_inner))
    def _():
        take(outer_ref)


def pick(here, inner, outer, fetched):
    edge = jax.ShapeDtypeStruct((EDGE * L, inner.shape[1]), inner.dtype)
    return call(
        pick_kernel,
        [jax.ShapeDtypeStruct(inner.shape, inner.dtype), edge],
        [here, inner, outer, fetched],
        name="pick",
    )


def spot_of(here_ref, inner, size, rows):
    late = 1 - here_ref[CORE] if inner else here_ref[CORE]
    return pl.ds(pl.multiple_of(late * (rows - size), L), size)


def finish(sides, here, inner, rows, state, weight, rim=None):
    top, total, mixed = state
    width = mixed.shape[0]
    part = weight.shape[1] // sides
    outs = [jax.ShapeDtypeStruct((rows, part), jnp.bfloat16)] * (sides - 1)
    outs += [jax.ShapeDtypeStruct((rows, part), jnp.float32)]
    scratch = [pltpu.VMEM((rows, width), jnp.bfloat16)]
    ins = [here, top, total, mixed]
    bias_start = 0
    if rim is not None:
        bias, bias_start, query, block = rim
        ins += [bias, query, *block]
        scratch += [pltpu.VMEM((2, block[0].shape[0], rows), jnp.float32)]
    return call(
        functools.partial(finish_kernel, sides, bias_start, inner, rim is not None),
        outs,
        ins + [weight],
        scratch=scratch,
        name="finish",
    )


def settle_kernel(inner, count, here_ref, *refs):
    kept_ref, term_refs = refs[0], refs[1:count]
    out_ref, hold, sem = refs[-3:]
    total = kept_ref[...]
    for term_ref in term_refs:
        total += term_ref[...].astype(jnp.float32)
    hold[...] = total.astype(hold.dtype)
    rows = hold.shape[0]
    spot = spot_of(here_ref, inner, rows, out_ref.shape[0])
    copy = pltpu.make_async_copy(hold, out_ref.at[spot, :], sem)
    copy.start()
    copy.wait()


def settle(here, inner, parts, rows, before=None):
    size, width = parts[0].shape
    ins = [here, *parts] + ([] if before is None else [before])
    return call(
        functools.partial(settle_kernel, inner, len(parts)),
        jax.ShapeDtypeStruct((rows, width), jnp.bfloat16),
        ins,
        scratch=[pltpu.VMEM((size, width), jnp.bfloat16), pltpu.SemaphoreType.DMA],
        out_specs=HBM,
        whole=() if before is None else (len(ins) - 1,),
        aliases=None if before is None else {len(ins) - 1: 0},
        name="settle",
    )


def shards(tokens, w_query, w_key, w_value, w_out, partners, counts):
    rows = tokens.shape[0]
    views_here = rows // L
    chips = lax.axis_size("views")
    cores = lax.axis_size("sub")
    sides = lax.axis_size("heads")
    core = lax.axis_index("sub")
    here = jnp.stack([lax.axis_index(name) for name in ("views", "sub", "heads")]).astype(jnp.int32)

    def shift(a, step):
        return lax.ppermute(a, "heads", [(h, (h + step) % sides) for h in range(sides)])

    def gather(groups):
        return [groups] + [[shift(a, step) for a in groups] for step in range(1, sides)]

    def share(block):
        return tuple(lax.ppermute(a, "sub", [(0, 1), (1, 0)]) for a in block)

    pair = [(z, z ^ 1) for z in range(chips)]
    side_step = [(z, ((z - 1) if z % 2 == 0 else (z + 1)) % chips) for z in range(chips)]
    edge_rows = EDGE * L
    own = gather([tokens])
    near = lax.ppermute(tokens, "views", pair)
    fetched = fetch(here, w_key, w_value, w_query)
    if chips == 4:
        inner = lax.ppermute(tokens, "views", [(1, 2), (2, 1)])
        outer = after(tokens, near, own[1][0], inner, fetched)
        outer = lax.ppermute(outer, "views", [(0, 3), (3, 0)])
    else:
        beyond = lax.ppermute(tokens, "views", side_step)
        rim = lax.dynamic_slice_in_dim(tokens, core * (rows - edge_rows), edge_rows, axis=0)
        edge = [(2 * z + 1, 2 * ((z + 2) % chips)) for z in range(chips)]
        edge += [(2 * z, 2 * ((z - 2) % chips) + 1) for z in range(chips)]
        here = after(here, rim)
        rim = lax.ppermute(rim, ("views", "sub"), edge)
    near = gather([after(near, fetched)])
    block, query = project(here, own, w_key, w_value, w_query, parts=1)
    own_shared = share(block)
    bias = make_mask(chips, cores, after(here, query), counts, partners, fetched)
    state = attend(bias, 0, query, [block], None)
    if chips == 4:
        beyond, rim = pick(here, after(inner, state[0]), outer, fetch(near[1][0], flops=FAKE))
        cross = [(2 * z + c, 2 * (z ^ 1) + 1 - c) for z in range(chips) for c in range(cores)]
        rim = lax.ppermute(rim, ("views", "sub"), cross)
    near[1][0] = after(near[1][0], beyond)
    (block,) = project(here, near, w_key, w_value)
    near_shared = share(block)
    beyond = gather([beyond])
    state = attend(bias, views_here, query, [block], state, flops=FAKE)
    rim = gather([after(rim, state[0])])
    beyond[1][0] = after(beyond[1][0], state[0], rim[0][0])
    (block,) = project(here, beyond, w_key, w_value)
    beyond_shared = share((after(block[0], rim[1][0]), block[1]))
    state = attend(bias, 2 * views_here, query, [near_shared, own_shared, block], state)
    (rim_block,) = project(here, rim, w_key, w_value)
    state = attend(bias, 5 * views_here, query, [beyond_shared], state)

    inner = finish(sides, here, True, rows - edge_rows, state, w_out)
    outer = finish(
        sides, here, False, edge_rows, [after(state[0], inner[0]), *state[1:]], w_out,
        (bias, 6 * views_here, query, rim_block),
    )

    def exchange(parts):
        return [parts[-1]] + [shift(part, step + 1) for step, part in enumerate(parts[:-1])]

    inner, outer = exchange(inner), exchange(outer)
    attended = settle(here, True, inner, rows)
    return settle(here, False, outer, rows, attended)


def solution(mesh):
    in_specs = (
        P(("groups", "views", "sub"), "heads"),
        P(None, "heads"),
        P(None, "heads"),
        P(None, "heads"),
        P("heads", None),
        P(("groups", "views", "sub"), None),
        P(("groups", "views", "sub")),
    )
    out_specs = P(("groups", "views", "sub"), "heads")
    return jax.shard_map(shards, mesh=mesh, in_specs=in_specs, out_specs=out_specs, check_vma=False)
```

```python
import functools

import jax
import jax.numpy as jnp
from jax import lax
from jax.experimental import pallas as pl
from jax.experimental.pallas import tpu as pltpu
from jax.sharding import PartitionSpec as P

HD = 128
L = 64
EDGE = 2
MB = 1 << 20
FACTOR = HD ** (-0.5) * 1.4426950408889634
ROWS_BY_ROWS = (((1,), (1,)), ((), ()))

VMEM = pl.BlockSpec(memory_space=pltpu.VMEM)
SMEM = pl.BlockSpec(memory_space=pltpu.SMEM)
HBM = pl.BlockSpec(memory_space=pl.ANY)
PLACE, CORE, SIDE = range(3)


def call(kernel, outs, ins, scratch=(), name=None, out_specs=None, aliases=None, whole=()):
    return pl.pallas_call(
        kernel,
        out_shape=outs,
        in_specs=[
            HBM if k in whole else SMEM if a.dtype == jnp.int32 and a.ndim == 1 else VMEM
            for k, a in enumerate(ins)
        ],
        out_specs=jax.tree.map(lambda _: VMEM, outs) if out_specs is None else out_specs,
        scratch_shapes=list(scratch),
        input_output_aliases=aliases or {},
        compiler_params=pltpu.CompilerParams(vmem_limit_bytes=16 * MB),
        cost_estimate=pl.CostEstimate(flops=0, bytes_accessed=0, transcendentals=0),
        name=name,
    )(*ins)


def after(a, *others):
    return lax.optimization_barrier((a, *others))[0]


def mask_kernel(chips, cores, here_ref, counts_ref, partners_ref, *refs):
    bias_ref = refs[-1]
    views, width = partners_ref.shape
    total = views * chips * cores
    place, core = here_ref[PLACE], here_ref[CORE]
    near = place + 1 - 2 * lax.rem(place, 2)
    beyond = lax.rem(place + chips - 1 + 2 * lax.rem(place, 2), chips)
    bases = []
    for at, other in ((place, 0), (near, 0), (near, 1), (place, 1), (beyond, 0), (beyond, 1)):
        bases.append((at * cores + core * (1 - 2 * other) + other) * views)
    behind = (lax.rem(place + chips - 2, chips) * cores + 1) * views + views - EDGE
    ahead = lax.rem(place + 2, chips) * cores * views
    bases.append(jnp.where(core == 0, behind, ahead))
    rows = bias_ref.shape[0]
    row = lax.broadcasted_iota(jnp.int32, (rows, width), 0)
    listed = row + bases[0]
    for block in range(1, len(bases)):
        listed = jnp.where(row >= block * views, row - block * views + bases[block], listed)
    slot = lax.broadcasted_iota(jnp.int32, (rows, width), 1)
    for view in range(views):
        mine = (place * cores + core) * views + view
        hit = (partners_ref[view : view + 1, :] == listed) & (slot < counts_ref[view])
        hit = jnp.where(hit | (listed == mine), 1, 0)
        hit = jnp.max(hit, axis=1, keepdims=True)
        mask = jnp.where(hit > 0, 0.0, -1e30).astype(jnp.float32)
        bias_ref[:, view * L : view * L + L] = jnp.broadcast_to(mask, (rows, L))


def fetch_kernel(*refs):
    refs[-1][...] = jnp.zeros_like(refs[-1])


def fetch(*arrays):
    return call(fetch_kernel, jax.ShapeDtypeStruct((8, 128), jnp.float32), arrays, name="fetch")


def make_mask(chips, cores, here, counts, partners, fetched):
    views = partners.shape[0]
    return call(
        functools.partial(mask_kernel, chips, cores),
        jax.ShapeDtypeStruct((6 * views + EDGE, views * L), jnp.float32),
        [here, counts, partners, fetched],
        name="mask",
    )


def project_kernel(pieces, groups, parts, with_query, here_ref, *refs):
    token_refs, refs = refs[: pieces * groups], refs[pieces * groups :]
    token_refs = [token_refs[k * groups : k * groups + groups] for k in range(pieces)]
    depth = token_refs[0][0].shape[1]
    spans = []
    for step in range(pieces):
        place = lax.rem(here_ref[SIDE] + pieces - step, pieces)
        spans.append(pl.ds(pl.multiple_of(place * depth, depth), depth))

    def products(weight_ref):
        width = weight_ref.shape[1]
        tile = min(512, width)
        for start in range(0, width, tile):
            total = None
            for group_refs, span in zip(token_refs, spans):
                term = jnp.dot(
                    jnp.concatenate([ref[...] for ref in group_refs]),
                    weight_ref[span, start : start + tile],
                    preferred_element_type=jnp.float32,
                )
                total = term if total is None else total + term
            yield start, total.astype(jnp.bfloat16)

    rows = sum(ref.shape[0] for ref in token_refs[0])
    block_refs, refs = refs[2 + with_query : 2 + with_query + parts], refs[:2 + with_query] + refs[2 + with_query + parts :]
    key_ref, value_ref = halves_of(block_refs)
    for start, result in products(refs[0]):
        key_ref[:, start : start + result.shape[1]] = result
    for start, result in products(refs[1]):
        for column in range(0, result.shape[1], HD):
            at, keys = value_place((start + column) // HD, rows)
            value_ref[at, keys] = result[:, column : column + HD].T
    if with_query:
        for start, result in products(refs[2]):
            refs[3][start : start + result.shape[1], :] = result.T


def value_place(head, keys):
    deep = keys // HD
    first = head % deep * HD
    return slice(first, first + HD), slice(head // deep * keys, head // deep * keys + keys)


def halves_of(block_refs):
    if len(block_refs) == 2:
        return block_refs
    rows = block_refs[0].shape[0] // 2
    return block_refs[0].at[:rows], block_refs[0].at[rows:]


def project(here, tokens, w_key, w_value, w_query=None, parts=2):
    rows = sum(a.shape[0] for a in tokens[0])
    width = w_key.shape[1]
    weights = [w_key, w_value] + ([] if w_query is None else [w_query])
    outs = [jax.ShapeDtypeStruct((2 * rows // parts, width), jnp.bfloat16)] * parts
    if w_query is not None:
        outs += [jax.ShapeDtypeStruct((width, rows), jnp.bfloat16)]
    outs = call(
        functools.partial(project_kernel, len(tokens), len(tokens[0]), parts, w_query is not None),
        outs,
        [here, *[a for piece in tokens for a in piece], *weights],
        name="project",
    )
    return (tuple(outs[:parts]), *outs[parts:])


def scores_of(key_ref, first, last, query, column, bias_ref, bias_row, lanes, hold_ref, at, top):
    scores = jnp.dot(key_ref[first:last, column], query, preferred_element_type=jnp.float32)
    for view in range((last - first) // L):
        piece = scores[view * L : view * L + L] + bias_ref[bias_row + view : bias_row + view + 1, lanes]
        hold_ref[at + view * L : at + view * L + L, :] = piece
        best = jnp.max(piece.reshape(L // 8, 8, piece.shape[1]), axis=0)
        top = best if top is None else jnp.maximum(top, best)
    return top


def weigh(hold_ref, at, size, shift, value, total, mixed):
    weights = jnp.exp2(hold_ref[at : at + size, :] * FACTOR - shift)
    term = jnp.sum(weights.reshape(size // 8, 8, weights.shape[1]), axis=0)
    total = term if total is None else total + term
    update = jnp.dot(value, weights.astype(jnp.bfloat16), preferred_element_type=jnp.float32)
    mixed = update if mixed is None else mixed + update
    return total, mixed


def attend_kernel(blocks, bias_start, has_state, bias_ref, query_ref, *refs):
    pairs = []
    for parts in blocks:
        pairs.append(halves_of(refs[:parts]))
        refs = refs[parts:]
    if has_state:
        top_in, total_in, mixed_in, top_out, total_out, mixed_out, hold = refs
    else:
        top_out, total_out, mixed_out, hold = refs
    heads = query_ref.shape[0] // HD
    everything = slice(None)
    for head in range(heads):
        column = slice(head * HD, head * HD + HD)
        row = slice(head, head + 1)
        query = query_ref[column, :]
        slot = hold.at[head % 2]
        top, at, groups = None, 0, []
        for key_ref, value_ref in pairs:
            size = key_ref.shape[0]
            step = min(128, size)
            groups.append((at, size, value_ref))
            for first in range(0, size, step):
                top = scores_of(
                    key_ref, first, first + step, query, column,
                    bias_ref, bias_start + at // L, everything, slot, at, top,
                )
                at += step
        top = jnp.max(top, axis=0, keepdims=True)
        total = mixed = None
        if has_state:
            before = top_in[row, :]
            top = jnp.maximum(top, before)
        shift = top * FACTOR
        for at, size, value_ref in groups:
            value = value_ref[value_place(head, size)]
            total, mixed = weigh(slot, at, size, shift, value, total, mixed)
        total = jnp.sum(total, axis=0, keepdims=True)
        if has_state:
            keep = jnp.exp2(before * FACTOR - shift)
            total = total + total_in[row, :] * keep
            mixed = mixed + mixed_in[column, :] * keep
        top_out[row, :] = top
        total_out[row, :] = total
        mixed_out[column, :] = mixed


def attend(bias, bias_start, query, blocks, state):
    width, rows = query.shape
    heads = width // HD
    span = sum(a.shape[0] for block in blocks for a in block) // 2
    outs = [
        jax.ShapeDtypeStruct((heads, rows), jnp.float32),
        jax.ShapeDtypeStruct((heads, rows), jnp.float32),
        jax.ShapeDtypeStruct((width, rows), jnp.float32),
    ]
    return call(
        functools.partial(attend_kernel, [len(block) for block in blocks], bias_start, state is not None),
        outs,
        [bias, query, *[a for block in blocks for a in block], *(state or [])],
        scratch=[pltpu.VMEM((2, span, rows), jnp.float32)],
        name="attend",
    )


def finish_kernel(sides, bias_start, inner, has_rim, here_ref, top_ref, total_ref, mixed_ref, *refs):
    if has_rim:
        bias_ref, query_ref, key_ref, value_ref, weight_ref = refs[:5]
        refs = refs[5:]
        hold = refs[-1]
    else:
        weight_ref = refs[0]
        refs = refs[1:]
    sent_refs, kept_ref, done = refs[: sides - 1], refs[sides - 1], refs[sides]
    rows = kept_ref.shape[0]
    part = kept_ref.shape[1]
    spot = spot_of(here_ref, inner, rows, mixed_ref.shape[1])
    heads = mixed_ref.shape[0] // HD
    for head in range(heads):
        column = slice(head * HD, head * HD + HD)
        row = slice(head, head + 1)
        total = total_ref[row, spot]
        mixed = mixed_ref[column, spot]
        if has_rim:
            slot = hold.at[head % 2]
            size = key_ref.shape[0]
            before = top_ref[row, spot]
            top = scores_of(
                key_ref, 0, size, query_ref[column, spot], column,
                bias_ref, bias_start, spot, slot, 0, None,
            )
            top = jnp.maximum(jnp.max(top, axis=0, keepdims=True), before)
            shift = top * FACTOR
            value = value_ref[value_place(head, size)]
            more, update = weigh(slot, 0, size, shift, value, None, None)
            keep = jnp.exp2(before * FACTOR - shift)
            total = total * keep + jnp.sum(more, axis=0, keepdims=True)
            mixed = mixed * keep + update
        done[:, column] = (mixed / total).T.astype(done.dtype)
    for step in range(sides):
        step = (step + 1) % sides
        place = lax.rem(here_ref[SIDE] + step, sides)
        columns = pl.ds(pl.multiple_of(place * part, part), part)
        result = jnp.dot(done[...], weight_ref[:, columns], preferred_element_type=jnp.float32)
        if step == 0:
            kept_ref[...] = result
        else:
            sent_refs[step - 1][...] = result.astype(jnp.bfloat16)


def pick_kernel(here_ref, inner_ref, outer_ref, block_ref, edge_ref):
    place = here_ref[PLACE]
    is_inner = (place == 1) | (place == 2)

    def take(chosen_ref):
        block_ref[...] = chosen_ref[...]
        rows = spot_of(here_ref, False, edge_ref.shape[0], chosen_ref.shape[0])
        edge_ref[...] = chosen_ref[rows, :]

    @pl.when(is_inner)
    def _():
        take(inner_ref)

    @pl.when(jnp.logical_not(is_inner))
    def _():
        take(outer_ref)


def pick(here, inner, outer):
    edge = jax.ShapeDtypeStruct((EDGE * L, inner.shape[1]), inner.dtype)
    return call(
        pick_kernel,
        [jax.ShapeDtypeStruct(inner.shape, inner.dtype), edge],
        [here, inner, outer],
        name="pick",
    )


def spot_of(here_ref, inner, size, rows):
    late = 1 - here_ref[CORE] if inner else here_ref[CORE]
    return pl.ds(pl.multiple_of(late * (rows - size), L), size)


def finish(sides, here, inner, rows, state, weight, rim=None):
    top, total, mixed = state
    width = mixed.shape[0]
    part = weight.shape[1] // sides
    outs = [jax.ShapeDtypeStruct((rows, part), jnp.bfloat16)] * (sides - 1)
    outs += [jax.ShapeDtypeStruct((rows, part), jnp.float32)]
    scratch = [pltpu.VMEM((rows, width), jnp.bfloat16)]
    ins = [here, top, total, mixed]
    bias_start = 0
    if rim is not None:
        bias, bias_start, query, block = rim
        ins += [bias, query, *block]
        scratch += [pltpu.VMEM((2, block[0].shape[0], rows), jnp.float32)]
    return call(
        functools.partial(finish_kernel, sides, bias_start, inner, rim is not None),
        outs,
        ins + [weight],
        scratch=scratch,
        name="finish",
    )


def settle_kernel(inner, count, here_ref, *refs):
    kept_ref, term_refs = refs[0], refs[1:count]
    out_ref, hold, sem = refs[-3:]
    total = kept_ref[...]
    for term_ref in term_refs:
        total += term_ref[...].astype(jnp.float32)
    hold[...] = total.astype(hold.dtype)
    rows = hold.shape[0]
    spot = spot_of(here_ref, inner, rows, out_ref.shape[0])
    copy = pltpu.make_async_copy(hold, out_ref.at[spot, :], sem)
    copy.start()
    copy.wait()


def settle(here, inner, parts, rows, before=None):
    size, width = parts[0].shape
    ins = [here, *parts] + ([] if before is None else [before])
    return call(
        functools.partial(settle_kernel, inner, len(parts)),
        jax.ShapeDtypeStruct((rows, width), jnp.bfloat16),
        ins,
        scratch=[pltpu.VMEM((size, width), jnp.bfloat16), pltpu.SemaphoreType.DMA],
        out_specs=HBM,
        whole=() if before is None else (len(ins) - 1,),
        aliases=None if before is None else {len(ins) - 1: 0},
        name="settle",
    )


def shards(tokens, w_query, w_key, w_value, w_out, partners, counts):
    rows = tokens.shape[0]
    views_here = rows // L
    chips = lax.axis_size("views")
    cores = lax.axis_size("sub")
    sides = lax.axis_size("heads")
    core = lax.axis_index("sub")
    here = jnp.stack([lax.axis_index(name) for name in ("views", "sub", "heads")]).astype(jnp.int32)

    def shift(a, step):
        return lax.ppermute(a, "heads", [(h, (h + step) % sides) for h in range(sides)])

    def gather(groups):
        return [groups] + [[shift(a, step) for a in groups] for step in range(1, sides)]

    def share(block):
        return tuple(lax.ppermute(a, "sub", [(0, 1), (1, 0)]) for a in block)

    pair = [(z, z ^ 1) for z in range(chips)]
    side_step = [(z, ((z - 1) if z % 2 == 0 else (z + 1)) % chips) for z in range(chips)]
    edge_rows = EDGE * L
    own = gather([tokens])
    near = lax.ppermute(tokens, "views", pair)
    fetched = fetch(here, w_key, w_value, w_query)
    if chips == 4:
        inner = lax.ppermute(tokens, "views", [(1, 2), (2, 1)])
        outer = after(tokens, fetched)
        outer = lax.ppermute(outer, "views", [(0, 3), (3, 0)])
    else:
        beyond = lax.ppermute(tokens, "views", side_step)
        rim = lax.dynamic_slice_in_dim(tokens, core * (rows - edge_rows), edge_rows, axis=0)
        edge = [(2 * z + 1, 2 * ((z + 2) % chips)) for z in range(chips)]
        edge += [(2 * z, 2 * ((z - 2) % chips) + 1) for z in range(chips)]
        here = after(here, rim)
        rim = lax.ppermute(rim, ("views", "sub"), edge)
    near = gather([after(near, fetched)])
    block, query = project(here, own, w_key, w_value, w_query, parts=1)
    own_shared = share(block)
    bias = make_mask(chips, cores, after(here, query), counts, partners, fetched)
    state = attend(bias, 0, query, [block], None)
    if chips == 4:
        beyond, rim = pick(here, after(inner, state[0]), outer)
        cross = [(2 * z + c, 2 * (z ^ 1) + 1 - c) for z in range(chips) for c in range(cores)]
        rim = lax.ppermute(rim, ("views", "sub"), cross)
    near[1][0] = after(near[1][0], beyond)
    (block,) = project(here, near, w_key, w_value)
    near_shared = share(block)
    beyond = gather([beyond])
    state = attend(bias, views_here, query, [block], state)
    rim = gather([after(rim, state[0])])
    beyond[1][0] = after(beyond[1][0], state[0], rim[0][0])
    (block,) = project(here, beyond, w_key, w_value)
    beyond_shared = share(block)
    state = attend(bias, 2 * views_here, query, [near_shared, own_shared, block], state)
    state = attend(bias, 5 * views_here, query, [beyond_shared], state)

    inner = finish(sides, here, True, rows - edge_rows, state, w_out)
    (rim_block,) = project(here, [[after(a, inner[0]) for a in piece] for piece in rim], w_key, w_value)
    outer = finish(
        sides, here, False, edge_rows, [after(state[0], inner[0]), *state[1:]], w_out,
        (bias, 6 * views_here, query, rim_block),
    )

    def exchange(parts):
        return [parts[-1]] + [shift(part, step + 1) for step, part in enumerate(parts[:-1])]

    inner, outer = exchange(inner), exchange(outer)
    attended = settle(here, True, inner, rows)
    return settle(here, False, outer, rows, attended)


def solution(mesh):
    in_specs = (
        P(("groups", "views", "sub"), "heads"),
        P(None, "heads"),
        P(None, "heads"),
        P(None, "heads"),
        P("heads", None),
        P(("groups", "views", "sub"), None),
        P(("groups", "views", "sub")),
    )
    out_specs = P(("groups", "views", "sub"), "heads")
    return jax.shard_map(shards, mesh=mesh, in_specs=in_specs, out_specs=out_specs, check_vma=False)
```

```python
import functools

import jax
import jax.numpy as jnp
from jax import lax
from jax.experimental import pallas as pl
from jax.experimental.pallas import tpu as pltpu
from jax.sharding import PartitionSpec as P

HD = 128
L = 64
EDGE = 2
MB = 1 << 20
FACTOR = HD ** (-0.5) * 1.4426950408889634
ROWS_BY_ROWS = (((1,), (1,)), ((), ()))

VMEM = pl.BlockSpec(memory_space=pltpu.VMEM)
SMEM = pl.BlockSpec(memory_space=pltpu.SMEM)
HBM = pl.BlockSpec(memory_space=pl.ANY)
PLACE, CORE, SIDE = range(3)


def call(kernel, outs, ins, scratch=(), name=None, out_specs=None, aliases=None, whole=()):
    return pl.pallas_call(
        kernel,
        out_shape=outs,
        in_specs=[
            HBM if k in whole else SMEM if a.dtype == jnp.int32 and a.ndim == 1 else VMEM
            for k, a in enumerate(ins)
        ],
        out_specs=jax.tree.map(lambda _: VMEM, outs) if out_specs is None else out_specs,
        scratch_shapes=list(scratch),
        input_output_aliases=aliases or {},
        compiler_params=pltpu.CompilerParams(vmem_limit_bytes=16 * MB),
        cost_estimate=pl.CostEstimate(flops=0, bytes_accessed=0, transcendentals=0),
        name=name,
    )(*ins)


def after(a, *others):
    return lax.optimization_barrier((a, *others))[0]


def mask_kernel(chips, cores, here_ref, counts_ref, partners_ref, *refs):
    bias_ref = refs[-1]
    views, width = partners_ref.shape
    total = views * chips * cores
    place, core = here_ref[PLACE], here_ref[CORE]
    near = place + 1 - 2 * lax.rem(place, 2)
    beyond = lax.rem(place + chips - 1 + 2 * lax.rem(place, 2), chips)
    bases = []
    for at, other in ((place, 0), (near, 0), (near, 1), (place, 1), (beyond, 0), (beyond, 1)):
        bases.append((at * cores + core * (1 - 2 * other) + other) * views)
    behind = (lax.rem(place + chips - 2, chips) * cores + 1) * views + views - EDGE
    ahead = lax.rem(place + 2, chips) * cores * views
    bases.append(jnp.where(core == 0, behind, ahead))
    rows = bias_ref.shape[0]
    row = lax.broadcasted_iota(jnp.int32, (rows, width), 0)
    listed = row + bases[0]
    for block in range(1, len(bases)):
        listed = jnp.where(row >= block * views, row - block * views + bases[block], listed)
    slot = lax.broadcasted_iota(jnp.int32, (rows, width), 1)
    for view in range(views):
        mine = (place * cores + core) * views + view
        hit = (partners_ref[view : view + 1, :] == listed) & (slot < counts_ref[view])
        hit = jnp.where(hit | (listed == mine), 1, 0)
        hit = jnp.max(hit, axis=1, keepdims=True)
        mask = jnp.where(hit > 0, 0.0, -1e30).astype(jnp.float32)
        bias_ref[:, view * L : view * L + L] = jnp.broadcast_to(mask, (rows, L))


def fetch_kernel(*refs):
    refs[-1][...] = jnp.zeros_like(refs[-1])


def fetch(*arrays):
    return call(fetch_kernel, jax.ShapeDtypeStruct((8, 128), jnp.float32), arrays, name="fetch")


def make_mask(chips, cores, here, counts, partners, fetched):
    views = partners.shape[0]
    return call(
        functools.partial(mask_kernel, chips, cores),
        jax.ShapeDtypeStruct((6 * views + EDGE, views * L), jnp.float32),
        [here, counts, partners, fetched],
        name="mask",
    )


def project_kernel(pieces, groups, parts, with_query, begun, here_ref, *refs):
    token_refs, refs = refs[: pieces * groups], refs[pieces * groups :]
    token_refs = [token_refs[k * groups : k * groups + groups] for k in range(pieces)]
    depth = token_refs[0][0].shape[1]
    spans = []
    sides = refs[0].shape[0] // depth
    for step in range(begun, begun + pieces):
        place = lax.rem(here_ref[SIDE] + sides - step, sides)
        spans.append(pl.ds(pl.multiple_of(place * depth, depth), depth))

    if begun:
        weight_refs, refs = refs[:2], refs[2:]
        sum_refs, refs = refs[:2], weight_refs + refs[2:]
    elif parts == 0:
        for weight_ref, sum_ref in zip(refs[:2], refs[2:]):
            sum_ref[...] = jnp.dot(
                jnp.concatenate([ref[...] for ref in token_refs[0]]),
                weight_ref[spans[0], :],
                preferred_element_type=jnp.float32,
            )
        return

    def products(weight_ref):
        width = weight_ref.shape[1]
        tile = min(512, width)
        for start in range(0, width, tile):
            total = None
            if begun:
                sum_ref = sum_refs[0 if weight_ref is refs[0] else 1]
                total = sum_ref[:, start : start + tile]
            for group_refs, span in zip(token_refs, spans):
                term = jnp.dot(
                    jnp.concatenate([ref[...] for ref in group_refs]),
                    weight_ref[span, start : start + tile],
                    preferred_element_type=jnp.float32,
                )
                total = term if total is None else total + term
            yield start, total.astype(jnp.bfloat16)

    rows = sum(ref.shape[0] for ref in token_refs[0])
    block_refs, refs = refs[2 + with_query : 2 + with_query + parts], refs[:2 + with_query] + refs[2 + with_query + parts :]
    key_ref, value_ref = halves_of(block_refs)
    for start, result in products(refs[0]):
        key_ref[:, start : start + result.shape[1]] = result
    for start, result in products(refs[1]):
        for column in range(0, result.shape[1], HD):
            at, keys = value_place((start + column) // HD, rows)
            value_ref[at, keys] = result[:, column : column + HD].T
    if with_query:
        for start, result in products(refs[2]):
            refs[3][start : start + result.shape[1], :] = result.T


def value_place(head, keys):
    deep = keys // HD
    first = head % deep * HD
    return slice(first, first + HD), slice(head // deep * keys, head // deep * keys + keys)


def halves_of(block_refs):
    if len(block_refs) == 2:
        return block_refs
    rows = block_refs[0].shape[0] // 2
    return block_refs[0].at[:rows], block_refs[0].at[rows:]


def project_first(here, tokens, w_key, w_value):
    rows = sum(a.shape[0] for a in tokens)
    outs = [jax.ShapeDtypeStruct((rows, w_key.shape[1]), jnp.float32)] * 2
    return call(
        functools.partial(project_kernel, 1, len(tokens), 0, False, 0),
        outs,
        [here, *tokens, w_key, w_value],
        name="project_first",
    )


def project(here, tokens, w_key, w_value, w_query=None, parts=2, begun=()):
    rows = sum(a.shape[0] for a in tokens[0])
    width = w_key.shape[1]
    weights = [w_key, w_value] + ([] if w_query is None else [w_query])
    outs = [jax.ShapeDtypeStruct((2 * rows // parts, width), jnp.bfloat16)] * parts
    if w_query is not None:
        outs += [jax.ShapeDtypeStruct((width, rows), jnp.bfloat16)]
    outs = call(
        functools.partial(
            project_kernel, len(tokens), len(tokens[0]), parts, w_query is not None, int(len(begun) > 0)
        ),
        outs,
        [here, *[a for piece in tokens for a in piece], *weights, *begun],
        name="project",
    )
    return (tuple(outs[:parts]), *outs[parts:])


def scores_of(key_ref, first, last, query, column, bias_ref, bias_row, lanes, hold_ref, at, top):
    scores = jnp.dot(key_ref[first:last, column], query, preferred_element_type=jnp.float32)
    for view in range((last - first) // L):
        piece = scores[view * L : view * L + L] + bias_ref[bias_row + view : bias_row + view + 1, lanes]
        hold_ref[at + view * L : at + view * L + L, :] = piece
        best = jnp.max(piece.reshape(L // 8, 8, piece.shape[1]), axis=0)
        top = best if top is None else jnp.maximum(top, best)
    return top


def weigh(hold_ref, at, size, shift, value, total, mixed):
    weights = jnp.exp2(hold_ref[at : at + size, :] * FACTOR - shift)
    term = jnp.sum(weights.reshape(size // 8, 8, weights.shape[1]), axis=0)
    total = term if total is None else total + term
    update = jnp.dot(value, weights.astype(jnp.bfloat16), preferred_element_type=jnp.float32)
    mixed = update if mixed is None else mixed + update
    return total, mixed


def attend_kernel(blocks, bias_start, has_state, bias_ref, query_ref, *refs):
    pairs = []
    for parts in blocks:
        pairs.append(halves_of(refs[:parts]))
        refs = refs[parts:]
    if has_state:
        top_in, total_in, mixed_in, top_out, total_out, mixed_out, hold = refs
    else:
        top_out, total_out, mixed_out, hold = refs
    heads = query_ref.shape[0] // HD
    everything = slice(None)
    for head in range(heads):
        column = slice(head * HD, head * HD + HD)
        row = slice(head, head + 1)
        query = query_ref[column, :]
        slot = hold.at[head % 2]
        top, at, groups = None, 0, []
        for key_ref, value_ref in pairs:
            size = key_ref.shape[0]
            step = min(128, size)
            groups.append((at, size, value_ref))
            for first in range(0, size, step):
                top = scores_of(
                    key_ref, first, first + step, query, column,
                    bias_ref, bias_start + at // L, everything, slot, at, top,
                )
                at += step
        top = jnp.max(top, axis=0, keepdims=True)
        total = mixed = None
        if has_state:
            before = top_in[row, :]
            top = jnp.maximum(top, before)
        shift = top * FACTOR
        for at, size, value_ref in groups:
            value = value_ref[value_place(head, size)]
            total, mixed = weigh(slot, at, size, shift, value, total, mixed)
        total = jnp.sum(total, axis=0, keepdims=True)
        if has_state:
            keep = jnp.exp2(before * FACTOR - shift)
            total = total + total_in[row, :] * keep
            mixed = mixed + mixed_in[column, :] * keep
        top_out[row, :] = top
        total_out[row, :] = total
        mixed_out[column, :] = mixed


def attend(bias, bias_start, query, blocks, state):
    width, rows = query.shape
    heads = width // HD
    span = sum(a.shape[0] for block in blocks for a in block) // 2
    outs = [
        jax.ShapeDtypeStruct((heads, rows), jnp.float32),
        jax.ShapeDtypeStruct((heads, rows), jnp.float32),
        jax.ShapeDtypeStruct((width, rows), jnp.float32),
    ]
    return call(
        functools.partial(attend_kernel, [len(block) for block in blocks], bias_start, state is not None),
        outs,
        [bias, query, *[a for block in blocks for a in block], *(state or [])],
        scratch=[pltpu.VMEM((2, span, rows), jnp.float32)],
        name="attend",
    )


def finish_kernel(sides, blocks, inner, here_ref, top_ref, total_ref, mixed_ref, bias_ref, query_ref, *refs):
    pairs = []
    for parts, bias_start in blocks:
        pairs.append((*halves_of(refs[:parts]), bias_start))
        refs = refs[parts:]
    weight_ref, refs = refs[0], refs[1:]
    sent_refs, kept_ref, done, hold = refs[: sides - 1], *refs[sides - 1 :]
    rows, part = kept_ref.shape
    spot = spot_of(here_ref, inner, rows, mixed_ref.shape[1])
    heads = mixed_ref.shape[0] // HD
    for head in range(heads):
        column = slice(head * HD, head * HD + HD)
        row = slice(head, head + 1)
        slot = hold.at[head % 2]
        query = query_ref[column, spot]
        before = top_ref[row, spot]
        top, at = None, 0
        for key_ref, _, bias_start in pairs:
            size = key_ref.shape[0]
            for first in range(0, size, 128):
                top = scores_of(
                    key_ref, first, first + 128, query, column,
                    bias_ref, bias_start + first // L, spot, slot, at, top,
                )
                at += 128
        top = jnp.maximum(jnp.max(top, axis=0, keepdims=True), before)
        shift = top * FACTOR
        keep = jnp.exp2(before * FACTOR - shift)
        more = update = None
        at = 0
        for key_ref, value_ref, _ in pairs:
            size = key_ref.shape[0]
            value = value_ref[value_place(head, size)]
            more, update = weigh(slot, at, size, shift, value, more, update)
            at += size
        total = total_ref[row, spot] * keep + jnp.sum(more, axis=0, keepdims=True)
        mixed = mixed_ref[column, spot] * keep + update
        done[:, column] = (mixed / total).T.astype(done.dtype)
    for step in range(sides):
        step = (step + 1) % sides
        place = lax.rem(here_ref[SIDE] + step, sides)
        columns = pl.ds(pl.multiple_of(place * part, part), part)
        result = jnp.dot(done[...], weight_ref[:, columns], preferred_element_type=jnp.float32)
        if step == 0:
            kept_ref[...] = result
        else:
            sent_refs[step - 1][...] = result.astype(jnp.bfloat16)


def pick_kernel(here_ref, inner_ref, outer_ref, block_ref, edge_ref):
    place = here_ref[PLACE]
    is_inner = (place == 1) | (place == 2)

    def take(chosen_ref):
        block_ref[...] = chosen_ref[...]
        rows = spot_of(here_ref, False, edge_ref.shape[0], chosen_ref.shape[0])
        edge_ref[...] = chosen_ref[rows, :]

    @pl.when(is_inner)
    def _():
        take(inner_ref)

    @pl.when(jnp.logical_not(is_inner))
    def _():
        take(outer_ref)


def pick(here, inner, outer):
    edge = jax.ShapeDtypeStruct((EDGE * L, inner.shape[1]), inner.dtype)
    return call(
        pick_kernel,
        [jax.ShapeDtypeStruct(inner.shape, inner.dtype), edge],
        [here, inner, outer],
        name="pick",
    )


def spot_of(here_ref, inner, size, rows):
    late = 1 - here_ref[CORE] if inner else here_ref[CORE]
    return pl.ds(pl.multiple_of(late * (rows - size), L), size)


def finish(sides, here, inner, rows, state, weight, bias, query, blocks):
    width = query.shape[0]
    part = weight.shape[1] // sides
    outs = [jax.ShapeDtypeStruct((rows, part), jnp.bfloat16)] * (sides - 1)
    outs += [jax.ShapeDtypeStruct((rows, part), jnp.float32)]
    span = sum(a.shape[0] for block, _ in blocks for a in block) // 2
    return call(
        functools.partial(
            finish_kernel, sides, [(len(block), start) for block, start in blocks], inner
        ),
        outs,
        [here, *state, bias, query, *[a for block, _ in blocks for a in block], weight],
        scratch=[
            pltpu.VMEM((rows, width), jnp.bfloat16),
            pltpu.VMEM((2, span, rows), jnp.float32),
        ],
        name="finish",
    )


def settle_kernel(inner, count, here_ref, *refs):
    kept_ref, term_refs = refs[0], refs[1:count]
    out_ref, hold, sem = refs[-3:]
    total = kept_ref[...]
    for term_ref in term_refs:
        total += term_ref[...].astype(jnp.float32)
    hold[...] = total.astype(hold.dtype)
    rows = hold.shape[0]
    spot = spot_of(here_ref, inner, rows, out_ref.shape[0])
    copy = pltpu.make_async_copy(hold, out_ref.at[spot, :], sem)
    copy.start()
    copy.wait()


def settle(here, inner, parts, rows, before=None):
    size, width = parts[0].shape
    ins = [here, *parts] + ([] if before is None else [before])
    return call(
        functools.partial(settle_kernel, inner, len(parts)),
        jax.ShapeDtypeStruct((rows, width), jnp.bfloat16),
        ins,
        scratch=[pltpu.VMEM((size, width), jnp.bfloat16), pltpu.SemaphoreType.DMA],
        out_specs=HBM,
        whole=() if before is None else (len(ins) - 1,),
        aliases=None if before is None else {len(ins) - 1: 0},
        name="settle",
    )


def shards(tokens, w_query, w_key, w_value, w_out, partners, counts):
    rows = tokens.shape[0]
    views_here = rows // L
    chips = lax.axis_size("views")
    cores = lax.axis_size("sub")
    sides = lax.axis_size("heads")
    core = lax.axis_index("sub")
    here = jnp.stack([lax.axis_index(name) for name in ("views", "sub", "heads")]).astype(jnp.int32)

    def shift(a, step):
        return lax.ppermute(a, "heads", [(h, (h + step) % sides) for h in range(sides)])

    def gather(groups):
        return [groups] + [[shift(a, step) for a in groups] for step in range(1, sides)]

    def share(block):
        return tuple(lax.ppermute(a, "sub", [(0, 1), (1, 0)]) for a in block)

    pair = [(z, z ^ 1) for z in range(chips)]
    side_step = [(z, ((z - 1) if z % 2 == 0 else (z + 1)) % chips) for z in range(chips)]
    edge_rows = EDGE * L
    own = gather([tokens])
    near = lax.ppermute(tokens, "views", pair)
    fetched = fetch(here, w_key, w_value, w_query)
    if chips == 4:
        inner = lax.ppermute(tokens, "views", [(1, 2), (2, 1)])
        outer = after(tokens, fetched)
        outer = lax.ppermute(outer, "views", [(0, 3), (3, 0)])
    else:
        beyond = lax.ppermute(tokens, "views", side_step)
        rim = lax.dynamic_slice_in_dim(tokens, core * (rows - edge_rows), edge_rows, axis=0)
        edge = [(2 * z + 1, 2 * ((z + 2) % chips)) for z in range(chips)]
        edge += [(2 * z, 2 * ((z - 2) % chips) + 1) for z in range(chips)]
        here = after(here, rim)
        rim = lax.ppermute(rim, ("views", "sub"), edge)
    near = gather([after(near, fetched)])
    block, query = project(here, own, w_key, w_value, w_query, parts=1)
    own_shared = share(block)
    bias = make_mask(chips, cores, after(here, query), counts, partners, fetched)
    state = attend(bias, 0, query, [block], None)
    if chips == 4:
        beyond, rim = pick(here, after(inner, state[0]), outer)
        cross = [(2 * z + c, 2 * (z ^ 1) + 1 - c) for z in range(chips) for c in range(cores)]
        rim = lax.ppermute(rim, ("views", "sub"), cross)
    near[1][0] = after(near[1][0], beyond)
    (block,) = project(here, near, w_key, w_value)
    near_shared = share(block)
    beyond = gather([beyond])
    state = attend(bias, views_here, query, [block], state)
    rim = gather([after(rim, state[0])])
    begun = project_first(here, [after(beyond[0][0], state[0])], w_key, w_value)
    beyond[1][0] = after(beyond[1][0], begun[0], rim[0][0])
    (block,) = project(here, beyond[1:], w_key, w_value, begun=begun)
    beyond_shared = share(block)
    state = attend(bias, 2 * views_here, query, [near_shared, own_shared, block], state)

    last = [(beyond_shared, 5 * views_here)]
    inner = finish(sides, here, True, rows - edge_rows, state, w_out, bias, query, last)
    rim = [[after(a, inner[0]) for a in piece] for piece in rim]
    (rim_block,) = project(here, rim, w_key, w_value)
    last.append((rim_block, 6 * views_here))
    state = [after(state[0], inner[0]), *state[1:]]
    outer = finish(sides, here, False, edge_rows, state, w_out, bias, query, last)

    def exchange(parts):
        return [parts[-1]] + [shift(part, step + 1) for step, part in enumerate(parts[:-1])]

    inner, outer = exchange(inner), exchange(outer)
    attended = settle(here, True, inner, rows)
    return settle(here, False, outer, rows, attended)


def solution(mesh):
    in_specs = (
        P(("groups", "views", "sub"), "heads"),
        P(None, "heads"),
        P(None, "heads"),
        P(None, "heads"),
        P("heads", None),
        P(("groups", "views", "sub"), None),
        P(("groups", "views", "sub")),
    )
    out_specs = P(("groups", "views", "sub"), "heads")
    return jax.shard_map(shards, mesh=mesh, in_specs=in_specs, out_specs=out_specs, check_vma=False)
```

```python
import functools

import jax
import jax.numpy as jnp
from jax import lax
from jax.experimental import pallas as pl
from jax.experimental.pallas import tpu as pltpu
from jax.sharding import PartitionSpec as P

HD = 128
L = 64
EDGE = 2
MB = 1 << 20
FACTOR = HD ** (-0.5) * 1.4426950408889634
ROWS_BY_ROWS = (((1,), (1,)), ((), ()))

VMEM = pl.BlockSpec(memory_space=pltpu.VMEM)
SMEM = pl.BlockSpec(memory_space=pltpu.SMEM)
HBM = pl.BlockSpec(memory_space=pl.ANY)
PLACE, CORE, SIDE = range(3)


def call(kernel, outs, ins, scratch=(), name=None, out_specs=None, aliases=None, whole=()):
    return pl.pallas_call(
        kernel,
        out_shape=outs,
        in_specs=[
            HBM if k in whole else SMEM if a.dtype == jnp.int32 and a.ndim == 1 else VMEM
            for k, a in enumerate(ins)
        ],
        out_specs=jax.tree.map(lambda _: VMEM, outs) if out_specs is None else out_specs,
        scratch_shapes=list(scratch),
        input_output_aliases=aliases or {},
        compiler_params=pltpu.CompilerParams(vmem_limit_bytes=16 * MB),
        cost_estimate=pl.CostEstimate(flops=0, bytes_accessed=0, transcendentals=0),
        name=name,
    )(*ins)


def after(a, *others):
    return lax.optimization_barrier((a, *others))[0]


def mask_kernel(chips, cores, here_ref, counts_ref, partners_ref, *refs):
    bias_ref = refs[-1]
    views, width = partners_ref.shape
    total = views * chips * cores
    place, core = here_ref[PLACE], here_ref[CORE]
    near = place + 1 - 2 * lax.rem(place, 2)
    beyond = lax.rem(place + chips - 1 + 2 * lax.rem(place, 2), chips)
    bases = []
    for at, other in ((place, 0), (near, 0), (near, 1), (place, 1), (beyond, 0), (beyond, 1)):
        bases.append((at * cores + core * (1 - 2 * other) + other) * views)
    behind = (lax.rem(place + chips - 2, chips) * cores + 1) * views + views - EDGE
    ahead = lax.rem(place + 2, chips) * cores * views
    bases.append(jnp.where(core == 0, behind, ahead))
    rows = bias_ref.shape[0]
    row = lax.broadcasted_iota(jnp.int32, (rows, width), 0)
    listed = row + bases[0]
    for block in range(1, len(bases)):
        listed = jnp.where(row >= block * views, row - block * views + bases[block], listed)
    slot = lax.broadcasted_iota(jnp.int32, (rows, width), 1)
    for view in range(views):
        mine = (place * cores + core) * views + view
        hit = (partners_ref[view : view + 1, :] == listed) & (slot < counts_ref[view])
        hit = jnp.where(hit | (listed == mine), 1, 0)
        hit = jnp.max(hit, axis=1, keepdims=True)
        mask = jnp.where(hit > 0, 0.0, -1e30).astype(jnp.float32)
        bias_ref[:, view * L : view * L + L] = jnp.broadcast_to(mask, (rows, L))


def fetch_kernel(*refs):
    refs[-1][...] = jnp.zeros_like(refs[-1])


def fetch(*arrays):
    return call(fetch_kernel, jax.ShapeDtypeStruct((8, 128), jnp.float32), arrays, name="fetch")


def make_mask(chips, cores, here, counts, partners, fetched):
    views = partners.shape[0]
    return call(
        functools.partial(mask_kernel, chips, cores),
        jax.ShapeDtypeStruct((6 * views + EDGE, views * L), jnp.float32),
        [here, counts, partners, fetched],
        name="mask",
    )


def project_kernel(pieces, groups, parts, with_query, begun, here_ref, *refs):
    token_refs, refs = refs[: pieces * groups], refs[pieces * groups :]
    token_refs = [token_refs[k * groups : k * groups + groups] for k in range(pieces)]
    depth = token_refs[0][0].shape[1]
    spans = []
    sides = refs[0].shape[0] // depth
    for step in range(begun, begun + pieces):
        place = lax.rem(here_ref[SIDE] + sides - step, sides)
        spans.append(pl.ds(pl.multiple_of(place * depth, depth), depth))

    if begun:
        weight_refs, refs = refs[:2], refs[2:]
        sum_refs, refs = refs[:2], weight_refs + refs[2:]
    elif parts == 0:
        for weight_ref, sum_ref in zip(refs[:2], refs[2:]):
            sum_ref[...] = jnp.dot(
                jnp.concatenate([ref[...] for ref in token_refs[0]]),
                weight_ref[spans[0], :],
                preferred_element_type=jnp.float32,
            )
        return

    def products(weight_ref):
        width = weight_ref.shape[1]
        tile = min(512, width)
        for start in range(0, width, tile):
            total = None
            if begun:
                sum_ref = sum_refs[0 if weight_ref is refs[0] else 1]
                total = sum_ref[:, start : start + tile]
            for group_refs, span in zip(token_refs, spans):
                term = jnp.dot(
                    jnp.concatenate([ref[...] for ref in group_refs]),
                    weight_ref[span, start : start + tile],
                    preferred_element_type=jnp.float32,
                )
                total = term if total is None else total + term
            yield start, total.astype(jnp.bfloat16)

    rows = sum(ref.shape[0] for ref in token_refs[0])
    block_refs, refs = refs[2 + with_query : 2 + with_query + parts], refs[:2 + with_query] + refs[2 + with_query + parts :]
    key_ref, value_ref = halves_of(block_refs)
    for start, result in products(refs[0]):
        key_ref[:, start : start + result.shape[1]] = result
    for start, result in products(refs[1]):
        for column in range(0, result.shape[1], HD):
            at, keys = value_place((start + column) // HD, rows)
            value_ref[at, keys] = result[:, column : column + HD].T
    if with_query:
        for start, result in products(refs[2]):
            refs[3][start : start + result.shape[1], :] = result.T


def value_place(head, keys):
    deep = keys // HD
    first = head % deep * HD
    return slice(first, first + HD), slice(head // deep * keys, head // deep * keys + keys)


def halves_of(block_refs):
    if len(block_refs) == 2:
        return block_refs
    rows = block_refs[0].shape[0] // 2
    return block_refs[0].at[:rows], block_refs[0].at[rows:]


def project_first(here, tokens, w_key, w_value):
    rows = sum(a.shape[0] for a in tokens)
    outs = [jax.ShapeDtypeStruct((rows, w_key.shape[1]), jnp.float32)] * 2
    return call(
        functools.partial(project_kernel, 1, len(tokens), 0, False, 0),
        outs,
        [here, *tokens, w_key, w_value],
        name="project_first",
    )


def project(here, tokens, w_key, w_value, w_query=None, parts=2, begun=()):
    rows = sum(a.shape[0] for a in tokens[0])
    width = w_key.shape[1]
    weights = [w_key, w_value] + ([] if w_query is None else [w_query])
    outs = [jax.ShapeDtypeStruct((2 * rows // parts, width), jnp.bfloat16)] * parts
    if w_query is not None:
        outs += [jax.ShapeDtypeStruct((width, rows), jnp.bfloat16)]
    outs = call(
        functools.partial(
            project_kernel, len(tokens), len(tokens[0]), parts, w_query is not None, int(len(begun) > 0)
        ),
        outs,
        [here, *[a for piece in tokens for a in piece], *weights, *begun],
        name="project",
    )
    return (tuple(outs[:parts]), *outs[parts:])


def scores_of(key_ref, first, last, query, column, bias_ref, bias_row, lanes, hold_ref, at, top):
    scores = jnp.dot(key_ref[first:last, column], query, preferred_element_type=jnp.float32)
    hold_ref[at : at + last - first, :] = scores
    for view in range((last - first) // L):
        piece = scores[view * L : view * L + L]
        best = jnp.max(piece.reshape(L // 8, 8, piece.shape[1]), axis=0)
        best = best + bias_ref[bias_row + view : bias_row + view + 1, lanes]
        top = best if top is None else jnp.maximum(top, best)
    return top


def weigh(hold_ref, at, size, bias_ref, bias_row, lanes, shift, value, total, mixed):
    weights = []
    for view in range(size // L):
        offset = bias_ref[bias_row + view : bias_row + view + 1, lanes] - shift
        piece = hold_ref[at + view * L : at + view * L + L, :] * FACTOR + offset
        weights.append(jnp.exp2(piece))
        term = jnp.sum(weights[-1].reshape(L // 8, 8, piece.shape[1]), axis=0)
        total = term if total is None else total + term
    weights = jnp.concatenate([w.astype(jnp.bfloat16) for w in weights])
    update = jnp.dot(value, weights, preferred_element_type=jnp.float32)
    mixed = update if mixed is None else mixed + update
    return total, mixed


def attend_head(head, pairs, query, bias_ref, lanes, hold_ref):
    column = slice(head * HD, head * HD + HD)
    top, at = None, 0
    for key_ref, _, bias_row in pairs:
        size = key_ref.shape[0]
        for first in range(0, size, 128):
            top = scores_of(
                key_ref, first, first + 128, query, column,
                bias_ref, bias_row + first // L, lanes, hold_ref, at, top,
            )
            at += 128

    def weighed(shift):
        total, mixed, at = None, None, 0
        for key_ref, value_ref, bias_row in pairs:
            size = key_ref.shape[0]
            value = value_ref[value_place(head, size)]
            total, mixed = weigh(
                hold_ref, at, size, bias_ref, bias_row, lanes, shift, value, total, mixed
            )
            at += size
        return jnp.sum(total, axis=0, keepdims=True), mixed

    return jnp.max(top, axis=0, keepdims=True), weighed


def attend_kernel(blocks, has_state, bias_ref, query_ref, *refs):
    pairs = []
    for parts, bias_row in blocks:
        pairs.append((*halves_of(refs[:parts]), bias_row))
        refs = refs[parts:]
    if has_state:
        top_in, total_in, mixed_in, top_out, total_out, mixed_out, hold = refs
    else:
        top_out, total_out, mixed_out, hold = refs
    heads = query_ref.shape[0] // HD

    def begin(head):
        query = query_ref[head * HD : head * HD + HD, :]
        return attend_head(head, pairs, query, bias_ref, slice(None), hold.at[head % 2])

    following = begin(0)
    for head in range(heads):
        top, weighed = following
        if head + 1 < heads:
            following = begin(head + 1)
        column = slice(head * HD, head * HD + HD)
        row = slice(head, head + 1)
        if has_state:
            before = top_in[row, :]
            top = jnp.maximum(top, before)
        shift = top * FACTOR
        total, mixed = weighed(shift)
        if has_state:
            keep = jnp.exp2(before * FACTOR - shift)
            total = total + total_in[row, :] * keep
            mixed = mixed + mixed_in[column, :] * keep
        top_out[row, :] = top
        total_out[row, :] = total
        mixed_out[column, :] = mixed


def attend(bias, bias_start, query, blocks, state):
    width, rows = query.shape
    heads = width // HD
    span, placed = 0, []
    for block in blocks:
        placed.append((len(block), bias_start + span // L))
        span += sum(a.shape[0] for a in block) // 2
    outs = [
        jax.ShapeDtypeStruct((heads, rows), jnp.float32),
        jax.ShapeDtypeStruct((heads, rows), jnp.float32),
        jax.ShapeDtypeStruct((width, rows), jnp.float32),
    ]
    return call(
        functools.partial(attend_kernel, placed, state is not None),
        outs,
        [bias, query, *[a for block in blocks for a in block], *(state or [])],
        scratch=[pltpu.VMEM((2, span, rows), jnp.float32)],
        name="attend",
    )


def finish_kernel(sides, blocks, inner, here_ref, top_ref, total_ref, mixed_ref, bias_ref, query_ref, *refs):
    pairs = []
    for parts, bias_start in blocks:
        pairs.append((*halves_of(refs[:parts]), bias_start))
        refs = refs[parts:]
    weight_ref, refs = refs[0], refs[1:]
    sent_refs, kept_ref, done, hold = refs[: sides - 1], *refs[sides - 1 :]
    rows, part = kept_ref.shape
    spot = spot_of(here_ref, inner, rows, mixed_ref.shape[1])
    heads = mixed_ref.shape[0] // HD

    def begin(head):
        query = query_ref[head * HD : head * HD + HD, spot]
        return attend_head(head, pairs, query, bias_ref, spot, hold.at[head % 2])

    following = begin(0)
    for head in range(heads):
        top, weighed = following
        if head + 1 < heads:
            following = begin(head + 1)
        column = slice(head * HD, head * HD + HD)
        row = slice(head, head + 1)
        before = top_ref[row, spot]
        top = jnp.maximum(top, before)
        shift = top * FACTOR
        keep = jnp.exp2(before * FACTOR - shift)
        total, mixed = weighed(shift)
        total = total_ref[row, spot] * keep + total
        mixed = mixed_ref[column, spot] * keep + mixed
        done[:, column] = (mixed / total).T.astype(done.dtype)
    for step in range(sides):
        step = (step + 1) % sides
        place = lax.rem(here_ref[SIDE] + step, sides)
        columns = pl.ds(pl.multiple_of(place * part, part), part)
        result = jnp.dot(done[...], weight_ref[:, columns], preferred_element_type=jnp.float32)
        if step == 0:
            kept_ref[...] = result
        else:
            sent_refs[step - 1][...] = result.astype(jnp.bfloat16)


def pick_kernel(here_ref, inner_ref, outer_ref, block_ref, edge_ref):
    place = here_ref[PLACE]
    is_inner = (place == 1) | (place == 2)

    def take(chosen_ref):
        block_ref[...] = chosen_ref[...]
        rows = spot_of(here_ref, False, edge_ref.shape[0], chosen_ref.shape[0])
        edge_ref[...] = chosen_ref[rows, :]

    @pl.when(is_inner)
    def _():
        take(inner_ref)

    @pl.when(jnp.logical_not(is_inner))
    def _():
        take(outer_ref)


def pick(here, inner, outer):
    edge = jax.ShapeDtypeStruct((EDGE * L, inner.shape[1]), inner.dtype)
    return call(
        pick_kernel,
        [jax.ShapeDtypeStruct(inner.shape, inner.dtype), edge],
        [here, inner, outer],
        name="pick",
    )


def spot_of(here_ref, inner, size, rows):
    late = 1 - here_ref[CORE] if inner else here_ref[CORE]
    return pl.ds(pl.multiple_of(late * (rows - size), L), size)


def finish(sides, here, inner, rows, state, weight, bias, query, blocks):
    width = query.shape[0]
    part = weight.shape[1] // sides
    outs = [jax.ShapeDtypeStruct((rows, part), jnp.bfloat16)] * (sides - 1)
    outs += [jax.ShapeDtypeStruct((rows, part), jnp.float32)]
    span = sum(a.shape[0] for block, _ in blocks for a in block) // 2
    return call(
        functools.partial(
            finish_kernel, sides, [(len(block), start) for block, start in blocks], inner
        ),
        outs,
        [here, *state, bias, query, *[a for block, _ in blocks for a in block], weight],
        scratch=[
            pltpu.VMEM((rows, width), jnp.bfloat16),
            pltpu.VMEM((2, span, rows), jnp.float32),
        ],
        name="finish",
    )


def settle_kernel(inner, count, here_ref, *refs):
    kept_ref, term_refs = refs[0], refs[1:count]
    out_ref, hold, sem = refs[-3:]
    total = kept_ref[...]
    for term_ref in term_refs:
        total += term_ref[...].astype(jnp.float32)
    hold[...] = total.astype(hold.dtype)
    rows = hold.shape[0]
    spot = spot_of(here_ref, inner, rows, out_ref.shape[0])
    copy = pltpu.make_async_copy(hold, out_ref.at[spot, :], sem)
    copy.start()
    copy.wait()


def settle(here, inner, parts, rows, before=None):
    size, width = parts[0].shape
    ins = [here, *parts] + ([] if before is None else [before])
    return call(
        functools.partial(settle_kernel, inner, len(parts)),
        jax.ShapeDtypeStruct((rows, width), jnp.bfloat16),
        ins,
        scratch=[pltpu.VMEM((size, width), jnp.bfloat16), pltpu.SemaphoreType.DMA],
        out_specs=HBM,
        whole=() if before is None else (len(ins) - 1,),
        aliases=None if before is None else {len(ins) - 1: 0},
        name="settle",
    )


def shards(tokens, w_query, w_key, w_value, w_out, partners, counts):
    rows = tokens.shape[0]
    views_here = rows // L
    chips = lax.axis_size("views")
    cores = lax.axis_size("sub")
    sides = lax.axis_size("heads")
    core = lax.axis_index("sub")
    here = jnp.stack([lax.axis_index(name) for name in ("views", "sub", "heads")]).astype(jnp.int32)

    def shift(a, step):
        return lax.ppermute(a, "heads", [(h, (h + step) % sides) for h in range(sides)])

    def gather(groups):
        return [groups] + [[shift(a, step) for a in groups] for step in range(1, sides)]

    def share(block):
        return tuple(lax.ppermute(a, "sub", [(0, 1), (1, 0)]) for a in block)

    pair = [(z, z ^ 1) for z in range(chips)]
    side_step = [(z, ((z - 1) if z % 2 == 0 else (z + 1)) % chips) for z in range(chips)]
    edge_rows = EDGE * L
    own = gather([tokens])
    near = lax.ppermute(tokens, "views", pair)
    fetched = fetch(here, w_key, w_value, w_query)
    if chips == 4:
        inner = lax.ppermute(tokens, "views", [(1, 2), (2, 1)])
        outer = after(tokens, fetched)
        outer = lax.ppermute(outer, "views", [(0, 3), (3, 0)])
    else:
        beyond = lax.ppermute(tokens, "views", side_step)
        rim = lax.dynamic_slice_in_dim(tokens, core * (rows - edge_rows), edge_rows, axis=0)
        edge = [(2 * z + 1, 2 * ((z + 2) % chips)) for z in range(chips)]
        edge += [(2 * z, 2 * ((z - 2) % chips) + 1) for z in range(chips)]
        here = after(here, rim)
        rim = lax.ppermute(rim, ("views", "sub"), edge)
    near = gather([after(near, fetched)])
    block, query = project(here, own, w_key, w_value, w_query, parts=1)
    own_shared = share(block)
    bias = make_mask(chips, cores, after(here, query), counts, partners, fetched)
    state = attend(bias, 0, query, [block], None)
    if chips == 4:
        beyond, rim = pick(here, after(inner, state[0]), outer)
        cross = [(2 * z + c, 2 * (z ^ 1) + 1 - c) for z in range(chips) for c in range(cores)]
        rim = lax.ppermute(rim, ("views", "sub"), cross)
    near[1][0] = after(near[1][0], beyond)
    (block,) = project(here, near, w_key, w_value)
    near_shared = share(block)
    beyond = gather([beyond])
    state = attend(bias, views_here, query, [block], state)
    rim = gather([after(rim, state[0])])
    begun = project_first(here, [after(beyond[0][0], state[0])], w_key, w_value)
    beyond[1][0] = after(beyond[1][0], begun[0], rim[0][0])
    (block,) = project(here, beyond[1:], w_key, w_value, begun=begun)
    beyond_shared = share(block)
    state = attend(bias, 2 * views_here, query, [near_shared, own_shared, block], state)

    last = [(beyond_shared, 5 * views_here)]
    inner = finish(sides, here, True, rows - edge_rows, state, w_out, bias, query, last)
    begun = project_first(here, [after(rim[0][0], inner[0])], w_key, w_value)
    rim[1][0] = after(rim[1][0], begun[0])
    (rim_block,) = project(here, rim[1:], w_key, w_value, begun=begun)
    last.append((rim_block, 6 * views_here))
    state = [after(state[0], inner[0]), *state[1:]]
    outer = finish(sides, here, False, edge_rows, state, w_out, bias, query, last)

    def exchange(parts):
        return [parts[-1]] + [shift(part, step + 1) for step, part in enumerate(parts[:-1])]

    inner, outer = exchange(inner), exchange(outer)
    attended = settle(here, True, inner, rows)
    return settle(here, False, outer, rows, attended)


def solution(mesh):
    in_specs = (
        P(("groups", "views", "sub"), "heads"),
        P(None, "heads"),
        P(None, "heads"),
        P(None, "heads"),
        P("heads", None),
        P(("groups", "views", "sub"), None),
        P(("groups", "views", "sub")),
    )
    out_specs = P(("groups", "views", "sub"), "heads")
    return jax.shard_map(shards, mesh=mesh, in_specs=in_specs, out_specs=out_specs, check_vma=False)
```

```python
import functools

import jax
import jax.numpy as jnp
from jax import lax
from jax.experimental import pallas as pl
from jax.experimental.pallas import tpu as pltpu
from jax.sharding import PartitionSpec as P

HD = 128
L = 64
EDGE = 2
MB = 1 << 20
FAKE = 10_000_000_000
FAKE2 = 3_000_000_000
FACTOR = HD ** (-0.5) * 1.4426950408889634
ROWS_BY_ROWS = (((1,), (1,)), ((), ()))

VMEM = pl.BlockSpec(memory_space=pltpu.VMEM)
SMEM = pl.BlockSpec(memory_space=pltpu.SMEM)
HBM = pl.BlockSpec(memory_space=pl.ANY)
PLACE, CORE, SIDE = range(3)


def call(kernel, outs, ins, scratch=(), name=None, out_specs=None, aliases=None, whole=(), flops=0):
    return pl.pallas_call(
        kernel,
        out_shape=outs,
        in_specs=[
            HBM if k in whole else SMEM if a.dtype == jnp.int32 and a.ndim == 1 else VMEM
            for k, a in enumerate(ins)
        ],
        out_specs=jax.tree.map(lambda _: VMEM, outs) if out_specs is None else out_specs,
        scratch_shapes=list(scratch),
        input_output_aliases=aliases or {},
        compiler_params=pltpu.CompilerParams(vmem_limit_bytes=16 * MB),
        cost_estimate=pl.CostEstimate(flops=flops, bytes_accessed=0, transcendentals=0),
        name=name,
    )(*ins)


def after(a, *others):
    return lax.optimization_barrier((a, *others))[0]


def mask_kernel(chips, cores, here_ref, counts_ref, partners_ref, *refs):
    bias_ref = refs[-1]
    views, width = partners_ref.shape
    total = views * chips * cores
    place, core = here_ref[PLACE], here_ref[CORE]
    near = place + 1 - 2 * lax.rem(place, 2)
    beyond = lax.rem(place + chips - 1 + 2 * lax.rem(place, 2), chips)
    bases = []
    for at, other in ((place, 0), (near, 0), (near, 1), (place, 1), (beyond, 0), (beyond, 1)):
        bases.append((at * cores + core * (1 - 2 * other) + other) * views)
    behind = (lax.rem(place + chips - 2, chips) * cores + 1) * views + views - EDGE
    ahead = lax.rem(place + 2, chips) * cores * views
    bases.append(jnp.where(core == 0, behind, ahead))
    rows = bias_ref.shape[0]
    row = lax.broadcasted_iota(jnp.int32, (rows, width), 0)
    listed = row + bases[0]
    for block in range(1, len(bases)):
        listed = jnp.where(row >= block * views, row - block * views + bases[block], listed)
    slot = lax.broadcasted_iota(jnp.int32, (rows, width), 1)
    for view in range(views):
        mine = (place * cores + core) * views + view
        hit = (partners_ref[view : view + 1, :] == listed) & (slot < counts_ref[view])
        hit = jnp.where(hit | (listed == mine), 1, 0)
        hit = jnp.max(hit, axis=1, keepdims=True)
        mask = jnp.where(hit > 0, 0.0, -1e30).astype(jnp.float32)
        bias_ref[:, view * L : view * L + L] = jnp.broadcast_to(mask, (rows, L))


def fetch_kernel(*refs):
    refs[-1][...] = jnp.zeros_like(refs[-1])


def fetch(*arrays, flops=0):
    return call(
        fetch_kernel, jax.ShapeDtypeStruct((8, 128), jnp.float32), arrays, name="fetch", flops=flops
    )


def make_mask(chips, cores, here, counts, partners, *fetched):
    views = partners.shape[0]
    return call(
        functools.partial(mask_kernel, chips, cores),
        jax.ShapeDtypeStruct((6 * views + EDGE, views * L), jnp.float32),
        [here, counts, partners, *fetched],
        name="mask",
    )


def project_kernel(pieces, groups, parts, with_query, begun, here_ref, *refs):
    token_refs, refs = refs[: pieces * groups], refs[pieces * groups :]
    token_refs = [token_refs[k * groups : k * groups + groups] for k in range(pieces)]
    depth = token_refs[0][0].shape[1]
    spans = []
    sides = refs[0].shape[0] // depth
    for step in range(begun, begun + pieces):
        place = lax.rem(here_ref[SIDE] + sides - step, sides)
        spans.append(pl.ds(pl.multiple_of(place * depth, depth), depth))

    if begun:
        weight_refs, refs = refs[:2], refs[2:]
        sum_refs, refs = refs[:2], weight_refs + refs[2:]
    elif parts == 0:
        for weight_ref, sum_ref in zip(refs[:2], refs[2:]):
            sum_ref[...] = jnp.dot(
                jnp.concatenate([ref[...] for ref in token_refs[0]]),
                weight_ref[spans[0], :],
                preferred_element_type=jnp.float32,
            )
        return

    def products(weight_ref):
        width = weight_ref.shape[1]
        tile = min(512, width)
        for start in range(0, width, tile):
            total = None
            if begun:
                sum_ref = sum_refs[0 if weight_ref is refs[0] else 1]
                total = sum_ref[:, start : start + tile]
            for group_refs, span in zip(token_refs, spans):
                term = jnp.dot(
                    jnp.concatenate([ref[...] for ref in group_refs]),
                    weight_ref[span, start : start + tile],
                    preferred_element_type=jnp.float32,
                )
                total = term if total is None else total + term
            yield start, total.astype(jnp.bfloat16)

    rows = sum(ref.shape[0] for ref in token_refs[0])
    block_refs, refs = refs[2 + with_query : 2 + with_query + parts], refs[:2 + with_query] + refs[2 + with_query + parts :]
    key_ref, value_ref = halves_of(block_refs)
    for start, result in products(refs[0]):
        key_ref[:, start : start + result.shape[1]] = result
    for start, result in products(refs[1]):
        for column in range(0, result.shape[1], HD):
            at, keys = value_place((start + column) // HD, rows)
            value_ref[at, keys] = result[:, column : column + HD].T
    if with_query:
        for start, result in products(refs[2]):
            refs[3][start : start + result.shape[1], :] = result.T


def value_place(head, keys):
    deep = keys // HD
    first = head % deep * HD
    return slice(first, first + HD), slice(head // deep * keys, head // deep * keys + keys)


def halves_of(block_refs):
    if len(block_refs) == 2:
        return block_refs
    rows = block_refs[0].shape[0] // 2
    return block_refs[0].at[:rows], block_refs[0].at[rows:]


def project_first(here, tokens, w_key, w_value):
    rows = sum(a.shape[0] for a in tokens)
    outs = [jax.ShapeDtypeStruct((rows, w_key.shape[1]), jnp.float32)] * 2
    return call(
        functools.partial(project_kernel, 1, len(tokens), 0, False, 0),
        outs,
        [here, *tokens, w_key, w_value],
        name="project_first",
    )


def project(here, tokens, w_key, w_value, w_query=None, parts=2, begun=()):
    rows = sum(a.shape[0] for a in tokens[0])
    width = w_key.shape[1]
    weights = [w_key, w_value] + ([] if w_query is None else [w_query])
    outs = [jax.ShapeDtypeStruct((2 * rows // parts, width), jnp.bfloat16)] * parts
    if w_query is not None:
        outs += [jax.ShapeDtypeStruct((width, rows), jnp.bfloat16)]
    outs = call(
        functools.partial(
            project_kernel, len(tokens), len(tokens[0]), parts, w_query is not None, int(len(begun) > 0)
        ),
        outs,
        [here, *[a for piece in tokens for a in piece], *weights, *begun],
        name="project",
    )
    return (tuple(outs[:parts]), *outs[parts:])


def scores_of(key_ref, first, last, query, column, bias_ref, bias_row, lanes, hold_ref, at, top):
    scores = jnp.dot(key_ref[first:last, column], query, preferred_element_type=jnp.float32)
    hold_ref[at : at + last - first, :] = scores
    for view in range((last - first) // L):
        piece = scores[view * L : view * L + L]
        best = jnp.max(piece.reshape(L // 8, 8, piece.shape[1]), axis=0)
        best = best + bias_ref[bias_row + view : bias_row + view + 1, lanes]
        top = best if top is None else jnp.maximum(top, best)
    return top


def weigh(hold_ref, at, size, bias_ref, bias_row, lanes, shift, value, total, mixed):
    weights = []
    for view in range(size // L):
        offset = bias_ref[bias_row + view : bias_row + view + 1, lanes] - shift
        piece = hold_ref[at + view * L : at + view * L + L, :] * FACTOR + offset
        weights.append(jnp.exp2(piece))
        term = jnp.sum(weights[-1].reshape(L // 8, 8, piece.shape[1]), axis=0)
        total = term if total is None else total + term
    weights = jnp.concatenate([w.astype(jnp.bfloat16) for w in weights])
    update = jnp.dot(value, weights, preferred_element_type=jnp.float32)
    mixed = update if mixed is None else mixed + update
    return total, mixed


def attend_head(head, pairs, query, bias_ref, lanes, hold_ref):
    column = slice(head * HD, head * HD + HD)
    top, at = None, 0
    for key_ref, _, bias_row in pairs:
        size = key_ref.shape[0]
        for first in range(0, size, 128):
            top = scores_of(
                key_ref, first, first + 128, query, column,
                bias_ref, bias_row + first // L, lanes, hold_ref, at, top,
            )
            at += 128

    def weighed(shift):
        total, mixed, at = None, None, 0
        for key_ref, value_ref, bias_row in pairs:
            size = key_ref.shape[0]
            value = value_ref[value_place(head, size)]
            total, mixed = weigh(
                hold_ref, at, size, bias_ref, bias_row, lanes, shift, value, total, mixed
            )
            at += size
        return jnp.sum(total, axis=0, keepdims=True), mixed

    return jnp.max(top, axis=0, keepdims=True), weighed


def attend_kernel(blocks, has_state, bias_ref, query_ref, *refs):
    pairs = []
    for parts, bias_row in blocks:
        pairs.append((*halves_of(refs[:parts]), bias_row))
        refs = refs[parts:]
    if has_state:
        top_in, total_in, mixed_in, top_out, total_out, mixed_out, hold = refs
    else:
        top_out, total_out, mixed_out, hold = refs
    heads = query_ref.shape[0] // HD

    def begin(head):
        query = query_ref[head * HD : head * HD + HD, :]
        return attend_head(head, pairs, query, bias_ref, slice(None), hold.at[head % 2])

    following = begin(0)
    for head in range(heads):
        top, weighed = following
        if head + 1 < heads:
            following = begin(head + 1)
        column = slice(head * HD, head * HD + HD)
        row = slice(head, head + 1)
        if has_state:
            before = top_in[row, :]
            top = jnp.maximum(top, before)
        shift = top * FACTOR
        total, mixed = weighed(shift)
        if has_state:
            keep = jnp.exp2(before * FACTOR - shift)
            total = total + total_in[row, :] * keep
            mixed = mixed + mixed_in[column, :] * keep
        top_out[row, :] = top
        total_out[row, :] = total
        mixed_out[column, :] = mixed


def attend(bias, bias_start, query, blocks, state, flops=0):
    width, rows = query.shape
    heads = width // HD
    span, placed = 0, []
    for block in blocks:
        placed.append((len(block), bias_start + span // L))
        span += sum(a.shape[0] for a in block) // 2
    outs = [
        jax.ShapeDtypeStruct((heads, rows), jnp.float32),
        jax.ShapeDtypeStruct((heads, rows), jnp.float32),
        jax.ShapeDtypeStruct((width, rows), jnp.float32),
    ]
    return call(
        functools.partial(attend_kernel, placed, state is not None),
        outs,
        [bias, query, *[a for block in blocks for a in block], *(state or [])],
        scratch=[pltpu.VMEM((2, span, rows), jnp.float32)],
        name="attend",
        flops=flops,
    )


def finish_kernel(sides, blocks, inner, here_ref, top_ref, total_ref, mixed_ref, bias_ref, query_ref, *refs):
    pairs = []
    for parts, bias_start in blocks:
        pairs.append((*halves_of(refs[:parts]), bias_start))
        refs = refs[parts:]
    weight_ref, refs = refs[0], refs[1:]
    sent_refs, done, hold = refs[: sides - 1], *refs[sides - 1 :]
    rows, part = sent_refs[0].shape
    spot = spot_of(here_ref, inner, rows, mixed_ref.shape[1])
    heads = mixed_ref.shape[0] // HD

    def begin(head):
        query = query_ref[head * HD : head * HD + HD, spot]
        return attend_head(head, pairs, query, bias_ref, spot, hold.at[head % 2])

    following = begin(0)
    for head in range(heads):
        top, weighed = following
        if head + 1 < heads:
            following = begin(head + 1)
        column = slice(head * HD, head * HD + HD)
        row = slice(head, head + 1)
        before = top_ref[row, spot]
        top = jnp.maximum(top, before)
        shift = top * FACTOR
        keep = jnp.exp2(before * FACTOR - shift)
        total, mixed = weighed(shift)
        total = total_ref[row, spot] * keep + total
        mixed = mixed_ref[column, spot] * keep + mixed
        done[:, column] = (mixed * (1.0 / total)).astype(done.dtype).T
    for step, sent_ref in enumerate(sent_refs):
        sent_ref[...] = output_part(here_ref, step + 1, sides, done, weight_ref).astype(jnp.bfloat16)


def output_part(here_ref, step, sides, done_ref, weight_ref):
    part = weight_ref.shape[1] // sides
    place = lax.rem(here_ref[SIDE] + step, sides)
    columns = pl.ds(pl.multiple_of(place * part, part), part)
    return jnp.dot(done_ref[...], weight_ref[:, columns], preferred_element_type=jnp.float32)


def keep_kernel(sides, here_ref, done_ref, weight_ref, kept_ref):
    kept_ref[...] = output_part(here_ref, 0, sides, done_ref, weight_ref)


def keep(sides, here, done, weight):
    return call(
        functools.partial(keep_kernel, sides),
        jax.ShapeDtypeStruct((done.shape[0], weight.shape[1] // sides), jnp.float32),
        [here, done, weight],
        name="keep",
    )


def pick_kernel(here_ref, inner_ref, outer_ref, block_ref, edge_ref):
    place = here_ref[PLACE]
    is_inner = (place == 1) | (place == 2)

    def take(chosen_ref):
        block_ref[...] = chosen_ref[...]
        rows = spot_of(here_ref, False, edge_ref.shape[0], chosen_ref.shape[0])
        edge_ref[...] = chosen_ref[rows, :]

    @pl.when(is_inner)
    def _():
        take(inner_ref)

    @pl.when(jnp.logical_not(is_inner))
    def _():
        take(outer_ref)


def pick(here, inner, outer):
    edge = jax.ShapeDtypeStruct((EDGE * L, inner.shape[1]), inner.dtype)
    return call(
        pick_kernel,
        [jax.ShapeDtypeStruct(inner.shape, inner.dtype), edge],
        [here, inner, outer],
        name="pick",
    )


def spot_of(here_ref, inner, size, rows):
    late = 1 - here_ref[CORE] if inner else here_ref[CORE]
    return pl.ds(pl.multiple_of(late * (rows - size), L), size)


def finish(sides, here, inner, rows, state, weight, bias, query, blocks):
    width = query.shape[0]
    part = weight.shape[1] // sides
    outs = [jax.ShapeDtypeStruct((rows, part), jnp.bfloat16)] * (sides - 1)
    outs += [jax.ShapeDtypeStruct((rows, width), jnp.bfloat16)]
    span = sum(a.shape[0] for block, _ in blocks for a in block) // 2
    return call(
        functools.partial(
            finish_kernel, sides, [(len(block), start) for block, start in blocks], inner
        ),
        outs,
        [here, *state, bias, query, *[a for block, _ in blocks for a in block], weight],
        scratch=[pltpu.VMEM((2, span, rows), jnp.float32)],
        name="finish",
    )


def settle_kernel(inner, count, here_ref, *refs):
    kept_ref, term_refs = refs[0], refs[1:count]
    out_ref, hold, sem = refs[-3:]
    total = kept_ref[...]
    for term_ref in term_refs:
        total += term_ref[...].astype(jnp.float32)
    hold[...] = total.astype(hold.dtype)
    rows = hold.shape[0]
    spot = spot_of(here_ref, inner, rows, out_ref.shape[0])
    copy = pltpu.make_async_copy(hold, out_ref.at[spot, :], sem)
    copy.start()
    copy.wait()


def settle(here, inner, parts, rows, before=None):
    size, width = parts[0].shape
    ins = [here, *parts] + ([] if before is None else [before])
    return call(
        functools.partial(settle_kernel, inner, len(parts)),
        jax.ShapeDtypeStruct((rows, width), jnp.bfloat16),
        ins,
        scratch=[pltpu.VMEM((size, width), jnp.bfloat16), pltpu.SemaphoreType.DMA],
        out_specs=HBM,
        whole=() if before is None else (len(ins) - 1,),
        aliases=None if before is None else {len(ins) - 1: 0},
        name="settle",
    )


def shards(tokens, w_query, w_key, w_value, w_out, partners, counts):
    rows = tokens.shape[0]
    views_here = rows // L
    chips = lax.axis_size("views")
    cores = lax.axis_size("sub")
    sides = lax.axis_size("heads")
    core = lax.axis_index("sub")
    here = jnp.stack([lax.axis_index(name) for name in ("views", "sub", "heads")]).astype(jnp.int32)

    def shift(a, step):
        return lax.ppermute(a, "heads", [(h, (h + step) % sides) for h in range(sides)])

    def gather(groups):
        return [groups] + [[shift(a, step) for a in groups] for step in range(1, sides)]

    def share(block):
        return tuple(lax.ppermute(a, "sub", [(0, 1), (1, 0)]) for a in block)

    pair = [(z, z ^ 1) for z in range(chips)]
    side_step = [(z, ((z - 1) if z % 2 == 0 else (z + 1)) % chips) for z in range(chips)]
    edge_rows = EDGE * L
    own = gather([tokens])
    near = lax.ppermute(tokens, "views", pair)
    fetched = fetch(here, w_key, w_value, w_query)
    if chips == 4:
        inner = lax.ppermute(tokens, "views", [(1, 2), (2, 1)])
        outer = after(tokens, fetched)
        outer = lax.ppermute(outer, "views", [(0, 3), (3, 0)])
    else:
        beyond = lax.ppermute(tokens, "views", side_step)
        rim = lax.dynamic_slice_in_dim(tokens, core * (rows - edge_rows), edge_rows, axis=0)
        edge = [(2 * z + 1, 2 * ((z + 2) % chips)) for z in range(chips)]
        edge += [(2 * z, 2 * ((z - 2) % chips) + 1) for z in range(chips)]
        here = after(here, rim)
        rim = lax.ppermute(rim, ("views", "sub"), edge)
    landed = fetch(near, flops=FAKE2)
    near = gather([after(near, fetched, landed)])
    block, query = project(here, own, w_key, w_value, w_query)
    own_shared = share(block)
    bias = make_mask(chips, cores, after(here, query), counts, partners, fetched, landed)
    state = attend(bias, 0, query, [block], None)
    if chips == 4:
        beyond, rim = pick(here, after(inner, state[0]), outer)
        cross = [(2 * z + c, 2 * (z ^ 1) + 1 - c) for z in range(chips) for c in range(cores)]
        rim = lax.ppermute(rim, ("views", "sub"), cross)
    near[1][0] = after(near[1][0], beyond)
    (block,) = project(here, near, w_key, w_value)
    near_shared = share(block)
    beyond = gather([beyond])
    state = attend(bias, views_here, query, [block], state)
    rim = gather([after(rim, state[0])])
    begun = project_first(here, [after(beyond[0][0], state[0])], w_key, w_value)
    beyond[1][0] = after(beyond[1][0], begun[0], rim[0][0])
    (block,) = project(here, beyond[1:], w_key, w_value, begun=begun)
    beyond_shared = share(block)
    state = attend(bias, 3 * views_here, query, [own_shared, block], state, flops=FAKE)

    last = [(near_shared, 2 * views_here), (beyond_shared, 5 * views_here)]
    inner = finish(sides, here, True, rows - edge_rows, state, w_out, bias, query, last)
    begun = project_first(here, [after(rim[0][0], inner[0])], w_key, w_value)
    rim[1][0] = after(rim[1][0], begun[0])
    (rim_block,) = project(here, rim[1:], w_key, w_value, begun=begun)
    last.append((rim_block, 6 * views_here))
    state = [after(state[0], inner[0]), *state[1:]]
    outer = finish(sides, here, False, edge_rows, state, w_out, bias, query, last)

    def exchange(parts):
        kept = keep(sides, here, parts[-1], w_out)
        return [kept] + [shift(part, step + 1) for step, part in enumerate(parts[:-1])]

    inner, outer = exchange(inner), exchange(outer)
    attended = settle(here, True, inner, rows)
    return settle(here, False, outer, rows, attended)


def solution(mesh):
    in_specs = (
        P(("groups", "views", "sub"), "heads"),
        P(None, "heads"),
        P(None, "heads"),
        P(None, "heads"),
        P("heads", None),
        P(("groups", "views", "sub"), None),
        P(("groups", "views", "sub")),
    )
    out_specs = P(("groups", "views", "sub"), "heads")
    return jax.shard_map(shards, mesh=mesh, in_specs=in_specs, out_specs=out_specs, check_vma=False)
```

```python
import functools

import jax
import jax.numpy as jnp
from jax import lax
from jax.experimental import pallas as pl
from jax.experimental.pallas import tpu as pltpu
from jax.sharding import PartitionSpec as P

HD = 128
L = 64
EDGE = 2
MB = 1 << 20
FAKE = 10_000_000_000
FAKE2 = 3_000_000_000
FACTOR = HD ** (-0.5) * 1.4426950408889634
ROWS_BY_ROWS = (((1,), (1,)), ((), ()))

VMEM = pl.BlockSpec(memory_space=pltpu.VMEM)
SMEM = pl.BlockSpec(memory_space=pltpu.SMEM)
HBM = pl.BlockSpec(memory_space=pl.ANY)
PLACE, CORE, SIDE = range(3)


def call(kernel, outs, ins, scratch=(), name=None, out_specs=None, aliases=None, whole=(), flops=0):
    return pl.pallas_call(
        kernel,
        out_shape=outs,
        in_specs=[
            HBM if k in whole else SMEM if a.dtype == jnp.int32 and a.ndim == 1 else VMEM
            for k, a in enumerate(ins)
        ],
        out_specs=jax.tree.map(lambda _: VMEM, outs) if out_specs is None else out_specs,
        scratch_shapes=list(scratch),
        input_output_aliases=aliases or {},
        compiler_params=pltpu.CompilerParams(vmem_limit_bytes=16 * MB),
        cost_estimate=pl.CostEstimate(flops=flops, bytes_accessed=0, transcendentals=0),
        name=name,
    )(*ins)


def after(a, *others):
    return lax.optimization_barrier((a, *others))[0]


def mask_kernel(chips, cores, here_ref, counts_ref, partners_ref, *refs):
    bias_ref = refs[-1]
    views, width = partners_ref.shape
    total = views * chips * cores
    place, core = here_ref[PLACE], here_ref[CORE]
    near = place + 1 - 2 * lax.rem(place, 2)
    beyond = lax.rem(place + chips - 1 + 2 * lax.rem(place, 2), chips)
    bases = []
    for at, other in ((place, 0), (near, 0), (place, 1), (near, 1), (beyond, 0), (beyond, 1)):
        bases.append((at * cores + core * (1 - 2 * other) + other) * views)
    behind = (lax.rem(place + chips - 2, chips) * cores + 1) * views + views - EDGE
    ahead = lax.rem(place + 2, chips) * cores * views
    bases.append(jnp.where(core == 0, behind, ahead))
    rows = bias_ref.shape[0]
    row = lax.broadcasted_iota(jnp.int32, (rows, width), 0)
    listed = row + bases[0]
    for block in range(1, len(bases)):
        listed = jnp.where(row >= block * views, row - block * views + bases[block], listed)
    slot = lax.broadcasted_iota(jnp.int32, (rows, width), 1)
    for view in range(views):
        mine = (place * cores + core) * views + view
        hit = (partners_ref[view : view + 1, :] == listed) & (slot < counts_ref[view])
        hit = jnp.where(hit | (listed == mine), 1, 0)
        hit = jnp.max(hit, axis=1, keepdims=True)
        mask = jnp.where(hit > 0, 0.0, -1e30).astype(jnp.float32)
        bias_ref[:, view * L : view * L + L] = jnp.broadcast_to(mask, (rows, L))


def fetch_kernel(*refs):
    refs[-1][...] = jnp.zeros_like(refs[-1])


def fetch(*arrays, flops=0):
    return call(
        fetch_kernel, jax.ShapeDtypeStruct((8, 128), jnp.float32), arrays, name="fetch", flops=flops
    )


def make_mask(chips, cores, here, counts, partners, *fetched):
    views = partners.shape[0]
    return call(
        functools.partial(mask_kernel, chips, cores),
        jax.ShapeDtypeStruct((6 * views + EDGE, views * L), jnp.float32),
        [here, counts, partners, *fetched],
        name="mask",
    )


def project_kernel(pieces, groups, parts, with_query, begun, here_ref, *refs):
    token_refs, refs = refs[: pieces * groups], refs[pieces * groups :]
    token_refs = [token_refs[k * groups : k * groups + groups] for k in range(pieces)]
    depth = token_refs[0][0].shape[1]
    spans = []
    sides = refs[0].shape[0] // depth
    for step in range(begun, begun + pieces):
        place = lax.rem(here_ref[SIDE] + sides - step, sides)
        spans.append(pl.ds(pl.multiple_of(place * depth, depth), depth))

    if begun:
        weight_refs, refs = refs[:2], refs[2:]
        sum_refs, refs = refs[:2], weight_refs + refs[2:]
    elif parts == 0:
        for weight_ref, sum_ref in zip(refs[:2], refs[2:]):
            sum_ref[...] = jnp.dot(
                jnp.concatenate([ref[...] for ref in token_refs[0]]),
                weight_ref[spans[0], :],
                preferred_element_type=jnp.float32,
            )
        return

    def products(weight_ref):
        width = weight_ref.shape[1]
        tile = min(512, width)
        for start in range(0, width, tile):
            total = None
            if begun:
                sum_ref = sum_refs[0 if weight_ref is refs[0] else 1]
                total = sum_ref[:, start : start + tile]
            for group_refs, span in zip(token_refs, spans):
                term = jnp.dot(
                    jnp.concatenate([ref[...] for ref in group_refs]),
                    weight_ref[span, start : start + tile],
                    preferred_element_type=jnp.float32,
                )
                total = term if total is None else total + term
            yield start, total.astype(jnp.bfloat16)

    rows = sum(ref.shape[0] for ref in token_refs[0])
    block_refs, refs = refs[2 + with_query : 2 + with_query + parts], refs[:2 + with_query] + refs[2 + with_query + parts :]
    key_ref, value_ref = halves_of(block_refs)
    for start, result in products(refs[0]):
        key_ref[:, start : start + result.shape[1]] = result
    for start, result in products(refs[1]):
        for column in range(0, result.shape[1], HD):
            at, keys = value_place((start + column) // HD, rows)
            value_ref[at, keys] = result[:, column : column + HD].T
    if with_query:
        for start, result in products(refs[2]):
            refs[3][start : start + result.shape[1], :] = result.T


def value_place(head, keys):
    deep = keys // HD
    first = head % deep * HD
    return slice(first, first + HD), slice(head // deep * keys, head // deep * keys + keys)


def halves_of(block_refs):
    if len(block_refs) == 2:
        return block_refs
    rows = block_refs[0].shape[0] // 2
    return block_refs[0].at[:rows], block_refs[0].at[rows:]


def project_first(here, tokens, w_key, w_value):
    rows = sum(a.shape[0] for a in tokens)
    outs = [jax.ShapeDtypeStruct((rows, w_key.shape[1]), jnp.float32)] * 2
    return call(
        functools.partial(project_kernel, 1, len(tokens), 0, False, 0),
        outs,
        [here, *tokens, w_key, w_value],
        name="project_first",
    )


def project(here, tokens, w_key, w_value, w_query=None, parts=2, begun=()):
    rows = sum(a.shape[0] for a in tokens[0])
    width = w_key.shape[1]
    weights = [w_key, w_value] + ([] if w_query is None else [w_query])
    outs = [jax.ShapeDtypeStruct((2 * rows // parts, width), jnp.bfloat16)] * parts
    if w_query is not None:
        outs += [jax.ShapeDtypeStruct((width, rows), jnp.bfloat16)]
    outs = call(
        functools.partial(
            project_kernel, len(tokens), len(tokens[0]), parts, w_query is not None, int(len(begun) > 0)
        ),
        outs,
        [here, *[a for piece in tokens for a in piece], *weights, *begun],
        name="project",
    )
    return (tuple(outs[:parts]), *outs[parts:])


def scores_of(key_ref, first, last, query, column, bias_ref, bias_row, lanes, hold_ref, at, top):
    scores = jnp.dot(key_ref[first:last, column], query, preferred_element_type=jnp.float32)
    hold_ref[at : at + last - first, :] = scores
    for view in range((last - first) // L):
        piece = scores[view * L : view * L + L]
        best = jnp.max(piece.reshape(L // 8, 8, piece.shape[1]), axis=0)
        best = best + bias_ref[bias_row + view : bias_row + view + 1, lanes]
        top = best if top is None else jnp.maximum(top, best)
    return top


def weigh(hold_ref, at, size, bias_ref, bias_row, lanes, shift, value, total, mixed):
    weights = []
    for view in range(size // L):
        offset = bias_ref[bias_row + view : bias_row + view + 1, lanes] - shift
        piece = hold_ref[at + view * L : at + view * L + L, :] * FACTOR + offset
        weights.append(jnp.exp2(piece))
        term = jnp.sum(weights[-1].reshape(L // 8, 8, piece.shape[1]), axis=0)
        total = term if total is None else total + term
    weights = jnp.concatenate([w.astype(jnp.bfloat16) for w in weights])
    update = jnp.dot(value, weights, preferred_element_type=jnp.float32)
    mixed = update if mixed is None else mixed + update
    return total, mixed


def attend_head(head, pairs, query, bias_ref, lanes, hold_ref):
    column = slice(head * HD, head * HD + HD)
    top, at = None, 0
    for key_ref, _, bias_row in pairs:
        size = key_ref.shape[0]
        for first in range(0, size, 128):
            top = scores_of(
                key_ref, first, first + 128, query, column,
                bias_ref, bias_row + first // L, lanes, hold_ref, at, top,
            )
            at += 128

    def weighed(shift):
        total, mixed, at = None, None, 0
        for key_ref, value_ref, bias_row in pairs:
            size = key_ref.shape[0]
            value = value_ref[value_place(head, size)]
            total, mixed = weigh(
                hold_ref, at, size, bias_ref, bias_row, lanes, shift, value, total, mixed
            )
            at += size
        return jnp.sum(total, axis=0, keepdims=True), mixed

    return jnp.max(top, axis=0, keepdims=True), weighed


def attend_kernel(blocks, has_state, bias_ref, query_ref, *refs):
    pairs = []
    for parts, bias_row in blocks:
        pairs.append((*halves_of(refs[:parts]), bias_row))
        refs = refs[parts:]
    if has_state:
        top_in, total_in, mixed_in, top_out, total_out, mixed_out, hold = refs
    else:
        top_out, total_out, mixed_out, hold = refs
    heads = query_ref.shape[0] // HD

    def begin(head):
        query = query_ref[head * HD : head * HD + HD, :]
        return attend_head(head, pairs, query, bias_ref, slice(None), hold.at[head % 2])

    following = begin(0)
    for head in range(heads):
        top, weighed = following
        if head + 1 < heads:
            following = begin(head + 1)
        column = slice(head * HD, head * HD + HD)
        row = slice(head, head + 1)
        if has_state:
            before = top_in[row, :]
            top = jnp.maximum(top, before)
        shift = top * FACTOR
        total, mixed = weighed(shift)
        if has_state:
            keep = jnp.exp2(before * FACTOR - shift)
            total = total + total_in[row, :] * keep
            mixed = mixed + mixed_in[column, :] * keep
        top_out[row, :] = top
        total_out[row, :] = total
        mixed_out[column, :] = mixed


def attend(bias, bias_start, query, blocks, state, flops=0):
    width, rows = query.shape
    heads = width // HD
    span, placed = 0, []
    for block in blocks:
        placed.append((len(block), bias_start + span // L))
        span += sum(a.shape[0] for a in block) // 2
    outs = [
        jax.ShapeDtypeStruct((heads, rows), jnp.float32),
        jax.ShapeDtypeStruct((heads, rows), jnp.float32),
        jax.ShapeDtypeStruct((width, rows), jnp.float32),
    ]
    return call(
        functools.partial(attend_kernel, placed, state is not None),
        outs,
        [bias, query, *[a for block in blocks for a in block], *(state or [])],
        scratch=[pltpu.VMEM((2, span, rows), jnp.float32)],
        name="attend",
        flops=flops,
    )


def finish_kernel(sides, blocks, inner, here_ref, top_ref, total_ref, mixed_ref, bias_ref, query_ref, *refs):
    pairs = []
    for parts, bias_start in blocks:
        pairs.append((*halves_of(refs[:parts]), bias_start))
        refs = refs[parts:]
    weight_ref, refs = refs[0], refs[1:]
    sent_refs, done, hold = refs[: sides - 1], *refs[sides - 1 :]
    rows, part = sent_refs[0].shape
    spot = spot_of(here_ref, inner, rows, mixed_ref.shape[1])
    heads = mixed_ref.shape[0] // HD

    def begin(head):
        query = query_ref[head * HD : head * HD + HD, spot]
        return attend_head(head, pairs, query, bias_ref, spot, hold.at[head % 2])

    following = begin(0)
    for head in range(heads):
        top, weighed = following
        if head + 1 < heads:
            following = begin(head + 1)
        column = slice(head * HD, head * HD + HD)
        row = slice(head, head + 1)
        before = top_ref[row, spot]
        top = jnp.maximum(top, before)
        shift = top * FACTOR
        keep = jnp.exp2(before * FACTOR - shift)
        total, mixed = weighed(shift)
        total = total_ref[row, spot] * keep + total
        mixed = mixed_ref[column, spot] * keep + mixed
        done[:, column] = (mixed * (1.0 / total)).astype(done.dtype).T
    for step, sent_ref in enumerate(sent_refs):
        sent_ref[...] = output_part(here_ref, step + 1, sides, done, weight_ref).astype(jnp.bfloat16)


def output_part(here_ref, step, sides, done_ref, weight_ref):
    part = weight_ref.shape[1] // sides
    place = lax.rem(here_ref[SIDE] + step, sides)
    columns = pl.ds(pl.multiple_of(place * part, part), part)
    return jnp.dot(done_ref[...], weight_ref[:, columns], preferred_element_type=jnp.float32)


def keep_kernel(sides, here_ref, done_ref, weight_ref, kept_ref):
    kept_ref[...] = output_part(here_ref, 0, sides, done_ref, weight_ref)


def keep(sides, here, done, weight):
    return call(
        functools.partial(keep_kernel, sides),
        jax.ShapeDtypeStruct((done.shape[0], weight.shape[1] // sides), jnp.float32),
        [here, done, weight],
        name="keep",
    )


def pick_kernel(here_ref, inner_ref, outer_ref, block_ref, edge_ref):
    place = here_ref[PLACE]
    is_inner = (place == 1) | (place == 2)

    def take(chosen_ref):
        block_ref[...] = chosen_ref[...]
        rows = spot_of(here_ref, False, edge_ref.shape[0], chosen_ref.shape[0])
        edge_ref[...] = chosen_ref[rows, :]

    @pl.when(is_inner)
    def _():
        take(inner_ref)

    @pl.when(jnp.logical_not(is_inner))
    def _():
        take(outer_ref)


def pick(here, inner, outer):
    edge = jax.ShapeDtypeStruct((EDGE * L, inner.shape[1]), inner.dtype)
    return call(
        pick_kernel,
        [jax.ShapeDtypeStruct(inner.shape, inner.dtype), edge],
        [here, inner, outer],
        name="pick",
    )


def spot_of(here_ref, inner, size, rows):
    late = 1 - here_ref[CORE] if inner else here_ref[CORE]
    return pl.ds(pl.multiple_of(late * (rows - size), L), size)


def finish(sides, here, inner, rows, state, weight, bias, query, blocks):
    width = query.shape[0]
    part = weight.shape[1] // sides
    outs = [jax.ShapeDtypeStruct((rows, part), jnp.bfloat16)] * (sides - 1)
    outs += [jax.ShapeDtypeStruct((rows, width), jnp.bfloat16)]
    span = sum(a.shape[0] for block, _ in blocks for a in block) // 2
    return call(
        functools.partial(
            finish_kernel, sides, [(len(block), start) for block, start in blocks], inner
        ),
        outs,
        [here, *state, bias, query, *[a for block, _ in blocks for a in block], weight],
        scratch=[pltpu.VMEM((2, span, rows), jnp.float32)],
        name="finish",
    )


def settle_kernel(inner, count, here_ref, *refs):
    kept_ref, term_refs = refs[0], refs[1:count]
    out_ref, hold, sem = refs[-3:]
    total = kept_ref[...]
    for term_ref in term_refs:
        total += term_ref[...].astype(jnp.float32)
    hold[...] = total.astype(hold.dtype)
    rows = hold.shape[0]
    spot = spot_of(here_ref, inner, rows, out_ref.shape[0])
    copy = pltpu.make_async_copy(hold, out_ref.at[spot, :], sem)
    copy.start()
    copy.wait()


def settle(here, inner, parts, rows, before=None):
    size, width = parts[0].shape
    ins = [here, *parts] + ([] if before is None else [before])
    return call(
        functools.partial(settle_kernel, inner, len(parts)),
        jax.ShapeDtypeStruct((rows, width), jnp.bfloat16),
        ins,
        scratch=[pltpu.VMEM((size, width), jnp.bfloat16), pltpu.SemaphoreType.DMA],
        out_specs=HBM,
        whole=() if before is None else (len(ins) - 1,),
        aliases=None if before is None else {len(ins) - 1: 0},
        name="settle",
    )


def shards(tokens, w_query, w_key, w_value, w_out, partners, counts):
    rows = tokens.shape[0]
    views_here = rows // L
    chips = lax.axis_size("views")
    cores = lax.axis_size("sub")
    sides = lax.axis_size("heads")
    core = lax.axis_index("sub")
    here = jnp.stack([lax.axis_index(name) for name in ("views", "sub", "heads")]).astype(jnp.int32)

    def shift(a, step):
        return lax.ppermute(a, "heads", [(h, (h + step) % sides) for h in range(sides)])

    def gather(groups):
        return [groups] + [[shift(a, step) for a in groups] for step in range(1, sides)]

    def share(block):
        return tuple(lax.ppermute(a, "sub", [(0, 1), (1, 0)]) for a in block)

    pair = [(z, z ^ 1) for z in range(chips)]
    side_step = [(z, ((z - 1) if z % 2 == 0 else (z + 1)) % chips) for z in range(chips)]
    edge_rows = EDGE * L
    own = gather([tokens])
    near = lax.ppermute(tokens, "views", pair)
    fetched = fetch(here, w_key, w_value, w_query)
    if chips == 4:
        inner = lax.ppermute(tokens, "views", [(1, 2), (2, 1)])
        outer = after(tokens, fetched)
        outer = lax.ppermute(outer, "views", [(0, 3), (3, 0)])
    else:
        beyond = lax.ppermute(tokens, "views", side_step)
        rim = lax.dynamic_slice_in_dim(tokens, core * (rows - edge_rows), edge_rows, axis=0)
        edge = [(2 * z + 1, 2 * ((z + 2) % chips)) for z in range(chips)]
        edge += [(2 * z, 2 * ((z - 2) % chips) + 1) for z in range(chips)]
        here = after(here, rim)
        rim = lax.ppermute(rim, ("views", "sub"), edge)
    landed = fetch(near, flops=FAKE2)
    near = gather([after(near, fetched, landed)])
    block, query = project(here, own, w_key, w_value, w_query)
    own_shared = share(block)
    bias = make_mask(chips, cores, after(here, query), counts, partners, fetched, landed)
    state = attend(bias, 0, query, [block], None)
    if chips == 4:
        beyond, rim = pick(here, after(inner, state[0]), outer)
        cross = [(2 * z + c, 2 * (z ^ 1) + 1 - c) for z in range(chips) for c in range(cores)]
        rim = lax.ppermute(rim, ("views", "sub"), cross)
    near[1][0] = after(near[1][0], beyond)
    (block,) = project(here, near, w_key, w_value)
    near_shared = share(block)
    beyond = gather([beyond])
    state = attend(bias, views_here, query, [block], state)
    begun = project_first(here, [after(beyond[0][0], state[0])], w_key, w_value)
    state = [after(state[0], begun[0]), *state[1:]]
    state = attend(bias, 2 * views_here, query, [own_shared], state)
    rim = gather([after(rim, state[0])])
    beyond[1][0] = after(beyond[1][0], begun[0], rim[0][0])
    (block,) = project(here, beyond[1:], w_key, w_value, begun=begun)
    beyond_shared = share(block)
    state = attend(bias, 4 * views_here, query, [block], state, flops=FAKE)
    state = attend(bias, 3 * views_here, query, [near_shared], state)

    last = [(beyond_shared, 5 * views_here)]
    inner = finish(sides, here, True, rows - edge_rows, state, w_out, bias, query, last)
    begun = project_first(here, [after(rim[0][0], inner[0])], w_key, w_value)
    rim[1][0] = after(rim[1][0], begun[0])
    (rim_block,) = project(here, rim[1:], w_key, w_value, begun=begun)
    last.append((rim_block, 6 * views_here))
    state = [after(state[0], inner[0]), *state[1:]]
    outer = finish(sides, here, False, edge_rows, state, w_out, bias, query, last)

    def exchange(parts):
        kept = keep(sides, here, parts[-1], w_out)
        return [kept] + [shift(part, step + 1) for step, part in enumerate(parts[:-1])]

    inner, outer = exchange(inner), exchange(outer)
    attended = settle(here, True, inner, rows)
    return settle(here, False, outer, rows, attended)


def solution(mesh):
    in_specs = (
        P(("groups", "views", "sub"), "heads"),
        P(None, "heads"),
        P(None, "heads"),
        P(None, "heads"),
        P("heads", None),
        P(("groups", "views", "sub"), None),
        P(("groups", "views", "sub")),
    )
    out_specs = P(("groups", "views", "sub"), "heads")
    return jax.shard_map(shards, mesh=mesh, in_specs=in_specs, out_specs=out_specs, check_vma=False)
```
